256 devices in a mesh: dp: 16 (over z_lo, y), tensor: 16 (over z_hi, x, core).
Axes of the slice: x: 4, y: 4, z: 8 (z_hi: 2, z_lo: 4; z = z_hi * 4 + z_lo), core: 2. Of those that a mesh axis runs over, the one named last changes fastest.
Arguments:
- activations: bfloat16 [6144, 8192], P('dp'), may hold values from -6 to 6
- out_grads: bfloat16 [6144, 16384], P('dp', 'tensor')
- left_stats: float32 [8192, 512], P('dp'), as said below
- old_roots: float32 [8192, 512], P('dp'), may hold values from -0.25 to 0.25
- refresh: int32 [4], replicated, may hold values from 0 to 15, as said below
Outputs:
- new_stats: float32 [8192, 512], P('dp')
- new_roots: float32 [8192, 512], P('dp')
- update: bfloat16 [8192, 16384], P('dp', 'tensor')
The draws below stay inside these ranges and needn't reach their ends.
Inputs may be any that keep to these rules, and one draw needn't show every extreme that they name: `left_stats`: each block of 512 rows is symmetric with a positive diagonal. `refresh`: 4 different block numbers, always including 0 and 15.
All inputs are finite; a program needn't handle non-finite values.
Results may differ from the reference program's by a relative error of at most 0.024.
Values may be sent and summed in bfloat16 or wider, within the bound.
A program may use at most 128 MiB of HBM per device.

```python
import math
import jax
import jax.numpy as jnp
from jax import lax

D = 8192
FF = 16384
B = 512
TOK_DEV = 384
ITERS = 6
TOKENS = 6144
NBLK = 16
REFRESH = 4
N_DP = 16


def draw_left_stats(key, part):
    key = jax.random.fold_in(key, 11)
    scale_key, noise_key = jax.random.split(key)
    log_low = math.log(0.1)
    log_high = math.log(10.0)
    scales = jnp.exp(0.5 * jax.random.uniform(scale_key, (NBLK, B), jnp.float32, log_low, log_high))
    noise_draw = jax.random.uniform(noise_key, (NBLK, B, B), jnp.float32, -1.0, 1.0)
    symmetric = 0.5 * (noise_draw + jnp.swapaxes(noise_draw, 1, 2))
    identity = jnp.eye(B, dtype=jnp.float32)
    coupling = identity + 0.8 / B * symmetric * (1.0 - identity)
    matrix = scales[:, :, None] * scales[:, None, :] * coupling
    return matrix.reshape(NBLK * B, B)


def column_scales(rise):
    position = jnp.arange(FF, dtype=jnp.float32) / (FF - 1)
    return jnp.sqrt(1.0 + rise * position)


def draw_out_grads(key, part):
    key = jax.random.fold_in(key, 5)
    noise_draw = jax.random.normal(key, (TOKENS, FF), jnp.float32)
    scales = column_scales(9.0)
    return (noise_draw * scales[None, :] * TOKENS ** (-0.5)).astype(jnp.bfloat16)


def draw_refresh(key, part):
    key = jax.random.fold_in(key, 7)
    middle = jax.random.permutation(key, NBLK - 2) + 1
    ends = jnp.array([NBLK - 1, 0], dtype=jnp.int32)
    return jnp.concatenate([ends, middle[:REFRESH - 2].astype(jnp.int32)]).astype(jnp.int32)


def strengthened(values, key, source, target, parts, factor):
    def block_of(dim):
        return (jnp.arange(values.shape[dim]) // (values.shape[dim] // parts)).reshape((-1,) + (1,) * (values.ndim - 1 - dim))

    one_side = jax.random.permutation(key, parts)[block_of(target)]
    far = (block_of(target) + parts // 2) % parts
    return jnp.where((block_of(source) == one_side) | (block_of(source) == far), factor * values, values)


def levels(stream_key, shape, cuts, low, largest):
    factor_of = 1.0
    for dim, blocks in cuts:
        heights = jax.random.uniform(jax.random.fold_in(jax.random.fold_in(stream_key, 6), dim), (blocks,), jnp.float32, low / len(cuts), largest / len(cuts))
        factor_of = factor_of * jnp.repeat(jnp.exp(heights), shape[dim] // blocks).reshape((-1,) + (1,) * (len(shape) - 1 - dim))
    return factor_of


def bell_draw(key, shape, width, limit, cuts=(), kind=jnp.bfloat16):
    result = width * jax.random.normal(key, shape, jnp.float32)
    if cuts:
        result = result * levels(key, shape, cuts, -0.22, 0.18)
    return jnp.clip(result, -limit, limit).astype(kind)


def bell_draw_with(key, shape, deviation, most, cuts, heavy, kind=jnp.bfloat16):
    values = deviation * jax.random.normal(key, shape, jnp.float32)
    if cuts:
        values = values * levels(key, shape, cuts, -0.22, 0.18)
    return jnp.clip(strengthened(values, jax.random.fold_in(key, 3), *heavy), -most, most).astype(kind)


def setup_inputs(seed: int = 0) -> dict:
    key_list = jax.random.split(jax.random.key(seed), 6)
    return {
        "activations": bell_draw_with(key_list[0], (TOKENS, D), 1.0, 6.0, ((0, 16),), (0, 1, 16, 2.0)),
        "out_grads": draw_out_grads(jax.random.fold_in(key_list[5], 71), 0),
        "left_stats": draw_left_stats(jax.random.fold_in(key_list[5], 71), 0),
        "old_roots": bell_draw(key_list[3], (D, B), B ** -0.5, 0.25, ((0, 16),), jnp.float32),
        "refresh": draw_refresh(jax.random.fold_in(key_list[5], 71), 0),
    }


STAT_DECAY = 0.8
TOP_PRECISION = lax.Precision.HIGHEST

def inverse_root(statistic):
    block_order = statistic.shape[0]
    identity = jnp.eye(block_order, dtype=jnp.float32)
    fro_norm = block_order * jnp.sqrt(jnp.mean(statistic * statistic) + 1e-06)
    newton_state = statistic / fro_norm
    iterate = fro_norm ** (-0.25) * identity
    for loop_index in range(ITERS):
        factor = (5.0 * identity - newton_state) / 4.0
        iterate = jnp.dot(iterate, factor, precision=TOP_PRECISION)
        if loop_index + 1 < ITERS:
            square = jnp.dot(factor, factor, precision=TOP_PRECISION)
            fourth = jnp.dot(square, square, precision=TOP_PRECISION)
            newton_state = jnp.dot(fourth, newton_state, precision=TOP_PRECISION)
    return iterate

def block_gram(rows_block):
    return jnp.dot(rows_block, rows_block.T, preferred_element_type=jnp.float32)

def block_update(matched):
    return jnp.dot(matched[0], matched[1], preferred_element_type=jnp.float32).astype(jnp.bfloat16)

def reference(activations, out_grads, left_stats, old_roots, refresh):
    act_groups = activations.reshape(N_DP, TOK_DEV, D)
    grad_groups = out_grads.reshape(N_DP, TOK_DEV, FF)

    def add_partial(running, matched):
        partial_value = jnp.dot(matched[0].T, matched[1], preferred_element_type=jnp.float32).astype(jnp.bfloat16)
        partial_value = lax.optimization_barrier(partial_value)
        return (running + partial_value.astype(jnp.float32), None)
    summed, unused = lax.scan(add_partial, jnp.zeros((D, FF), jnp.float32), (act_groups, grad_groups))
    reduced = summed.astype(jnp.bfloat16)
    grad_rows = reduced.reshape(NBLK, B, FF)
    gram_blocks = lax.map(block_gram, grad_rows)
    mix_weight = 1.0 / FF
    new_stats = STAT_DECAY * left_stats.reshape(NBLK, B, B) + mix_weight * gram_blocks
    fresh = lax.map(inverse_root, new_stats[refresh])
    new_roots = old_roots.reshape(NBLK, B, B).at[refresh].set(fresh)
    root_half = new_roots.astype(jnp.bfloat16)
    update = lax.map(block_update, (root_half, grad_rows))
    return (new_stats.reshape(D, B), new_roots.reshape(D, B), update.reshape(D, FF))
```

```python
import functools

import jax
import jax.numpy as jnp
from jax import lax
from jax.experimental import pallas as pl
from jax.experimental.pallas import tpu as pltpu
from jax.sharding import PartitionSpec as P

FF = 16384
ITERS = 6
STAT_DECAY = 0.8
NZ, NY, NX, NC = 4, 4, 4, 2
MESH = pl.DeviceIdType.MESH
WIDTHS = (256, 256, 256, 128, 128)
STARTS = tuple(sum(WIDTHS[:i]) for i in range(len(WIDTHS)))
ORDER = (2, 1, 3, 0)
BF16, F32 = jnp.bfloat16, jnp.float32


def _rem(a, n):
    return lax.rem(a + 2 * n, n)


def gradient_kernel(
    act, grad, red, gram_out,
    raw_near, raw_own, mine, at, gall, part, landed, own_part, gram, gsend, gcore, g1, g1land, g2, g2land,
    load_sem, az_send, az_recv, ax_send, ax_recv, ac_send, ac_recv,
    g_send, g_recv, p_send, p_recv, m_send, m_recv,
):
    tok = act.shape[0]
    blk = red.shape[0]
    row = blk // NX
    dp, tn = lax.axis_index("dp"), lax.axis_index("tensor")
    zl, y = dp // NY, lax.rem(dp, NY)
    zh, x, c = tn // (NX * NC), lax.rem(tn // NC, NX), lax.rem(tn, NC)
    z = zh * NZ + zl

    def device(dz=0, dy=0, dx=0, dc=0):
        pz = _rem(z + dz, 2 * NZ)
        return (
            lax.rem(pz, NZ) * NY + _rem(y + dy, NY),
            (pz // NZ) * NX * NC + _rem(x + dx, NX) * NC + _rem(c + dc, NC),
        )

    def remote(src, dst, send, recv, to):
        return pltpu.make_async_remote_copy(
            src_ref=src, dst_ref=dst, send_sem=send, recv_sem=recv, device_id=to, device_id_type=MESH
        )

    def arrival(dst, recv):
        return remote(dst, dst, recv, recv, device(dc=1))

    far = jnp.where(c == 0, 2, -2)
    waves = (jnp.where(c == 0, 2, 1), jnp.where(c == 0, 3, 0))
    hops = (1, -1, 2)
    near_load = []
    for w in range(2):
        for i, d in enumerate(hops):
            col = (_rem(zl + d, NZ) * NY + _rem(y + waves[w], NY)) * blk + x * row
            cp = pltpu.make_async_copy(
                act.at[:, pl.ds(pl.multiple_of(col, 128), row)], raw_near.at[w * 3 + i], load_sem.at[w * 3 + i]
            )
            cp.start()
            near_load.append(cp)
    own_load = []
    for r in range(NY):
        col = (zl * NY + _rem(y + r, NY)) * blk
        cp = pltpu.make_async_copy(act.at[:, pl.ds(pl.multiple_of(col, 128), blk)], raw_own.at[r], load_sem.at[6 + r])
        cp.start()
        own_load.append(cp)
    g_load = []
    for j, (s, wd) in enumerate(zip(STARTS, WIDTHS)):
        cp = pltpu.make_async_copy(grad.at[:, pl.ds(s, wd)], gall.at[j, pl.ds(0, tok), pl.ds(0, wd)], load_sem.at[10 + j])
        cp.start()
        g_load.append(cp)

    barrier = pltpu.get_barrier_semaphore()
    peers = [device(dz=d) for d in (1, -1, 2, -2, 4)]
    peers += [device(dy=d) for d in (1, 2, 3)] + [device(dx=d) for d in (1, 2, 3)] + [device(dc=1)]
    for p in peers:
        pl.semaphore_signal(barrier, inc=1, device_id=p, device_id_type=MESH)
    pl.semaphore_wait(barrier, len(peers))

    sent = []

    def g_slot(j, s):
        return gall.at[j, pl.ds(s * tok, tok), pl.ds(0, WIDTHS[j])]

    def g_copy(j, src, dst, way, to):
        return remote(g_slot(j, src), g_slot(j, dst), g_send.at[j, way], g_recv.at[j, dst], to)

    right, left = device(dz=1), device(dz=-1)

    def g_own(j):
        g_load[j].wait()
        pl.when(zl < NZ - 1)(lambda: g_copy(j, 0, 3, 0, right).start())
        pl.when(zl > 0)(lambda: g_copy(j, 0, 1, 1, left).start())

    def g_wait(j, s):
        arrival(g_slot(j, s), g_recv.at[j, s]).wait_recv()

    def g_relay(j):
        middle = (zl > 0) & (zl < NZ - 1)
        g_wait(j, 3)
        pl.when(middle)(lambda: g_copy(j, 3, 2, 2, right).start())
        g_wait(j, 1)
        pl.when(middle)(lambda: g_copy(j, 1, 2, 3, left).start())
        g_wait(j, 2)
        pl.when(zl == 1)(lambda: g_copy(j, 2, 3, 4, left).start())
        pl.when(zl == 2)(lambda: g_copy(j, 2, 1, 4, right).start())

    def g_drain(j):
        middle = (zl > 0) & (zl < NZ - 1)
        pl.when(zl < NZ - 1)(lambda: g_copy(j, 0, 3, 0, right).wait_send())
        pl.when(zl > 0)(lambda: g_copy(j, 0, 1, 1, left).wait_send())
        pl.when(middle)(lambda: g_copy(j, 3, 2, 2, right).wait_send())
        pl.when(middle)(lambda: g_copy(j, 1, 2, 3, left).wait_send())
        pl.when(middle)(lambda: g_copy(j, 2, 3, 4, left).wait_send())

    def at_piece(w, i, rows, count):
        slot = (-hops[i]) % NZ
        return at.at[waves[w], pl.ds(rows, count), pl.ds(slot * tok, tok)]

    my_rows = pl.multiple_of(x * row, 128)

    def a_send(w):
        for i, d in enumerate(hops):
            near_load[w * 3 + i].wait()
            mine[w * 3 + i] = raw_near[w * 3 + i].T
            cp = remote(
                mine.at[w * 3 + i], at_piece(w, i, my_rows, row), az_send.at[w * 3 + i], az_recv.at[w * 3 + i],
                device(dz=far if d == 2 else d),
            )
            cp.start()
            sent.append(cp)

    def a_share(w):
        for i in range(3):
            piece = at_piece(w, i, my_rows, row)
            arrival(piece, az_recv.at[w * 3 + i]).wait_recv()
            for k, d in enumerate((2, 1, 3)):
                cp = remote(piece, piece, ax_send.at[w * 3 + i, k], ax_recv.at[w * 3 + i, k], device(dx=d))
                cp.start()
                sent.append(cp)

    def a_core(w):
        for i in range(3):
            for k, d in enumerate((2, 1, 3)):
                rows = pl.multiple_of(_rem(x - d, NX) * row, 128)
                arrival(at_piece(w, i, rows, row), ax_recv.at[w * 3 + i, k]).wait_recv()
            piece = at_piece(w, i, 0, blk)
            cp = remote(piece, piece, ac_send.at[w * 3 + i], ac_recv.at[w * 3 + i], device(dc=1))
            cp.start()
            sent.append(cp)

    def a_wait(w):
        theirs = jnp.where(c == 0, (1, 0)[w], (2, 3)[w])
        for i in range(3):
            slot = (-hops[i]) % NZ
            arrival(at.at[theirs, pl.ds(0, blk), pl.ds(slot * tok, tok)], ac_recv.at[w * 3 + i]).wait_recv()

    def product(j, r):
        wd = WIDTHS[j]
        value = jnp.dot(at[r], gall[j, :, 0:wd], preferred_element_type=F32)
        if r == 0:
            own_part[j % 2, :, 0:wd] = value
        else:
            part[j, r - 1, :, 0:wd] = value.astype(BF16)
            cp = remote(
                part.at[j, r - 1, :, pl.ds(0, wd)], landed.at[j, NY - r - 1, :, pl.ds(0, wd)],
                p_send.at[j, r - 1], p_recv.at[j, NY - r - 1], device(dy=r),
            )
            cp.start()
            sent.append(cp)

    def finish(j):
        wd = WIDTHS[j]
        for k in (1, 0, 2):
            slot = landed.at[j, k, :, pl.ds(0, wd)]
            arrival(slot, p_recv.at[j, k]).wait_recv()
        total = own_part[j % 2, :, 0:wd] + landed[j, 0, :, 0:wd].astype(F32)
        total = total + landed[j, 1, :, 0:wd].astype(F32) + landed[j, 2, :, 0:wd].astype(F32)
        half = total.astype(BF16)
        red[:, STARTS[j]:STARTS[j] + wd] = half
        term = lax.dot_general(half, half, (((1,), (1,)), ((), ())), preferred_element_type=F32)
        if j == 0:
            gram[...] = term
        else:
            gram[...] += term

    a_send(0)
    g_own(0)
    a_send(1)
    g_own(1)
    a_share(0)
    for r in range(NY):
        own_load[r].wait()
        at[r, :, 0:tok] = raw_own[r].T
    a_share(1)
    g_relay(0)
    a_core(0)
    a_wait(0)
    product(0, 2)
    product(0, 1)
    g_own(2)
    g_relay(1)
    a_core(1)
    a_wait(1)
    product(0, 3)
    product(0, 0)
    n = len(WIDTHS)
    for j in range(1, n):
        if j + 2 < n:
            g_own(j + 2)
        if j > 1:
            g_relay(j)
        for r in ORDER:
            product(j, r)
        finish(j - 1)
    finish(n - 1)

    half_rows = blk // 2
    piece = half_rows // NX
    gsend[...] = gram[...].astype(BF16)
    other = remote(
        gsend.at[pl.ds(pl.multiple_of((1 - c) * half_rows, 128), half_rows)], gcore,
        m_send.at[0], m_recv.at[0], device(dc=1),
    )
    other.start()
    sent.append(other)
    other.wait_recv()
    mid = gram[pl.ds(pl.multiple_of(c * half_rows, 128), half_rows), :] + gcore[...].astype(F32)
    gram[0:half_rows, :] = mid
    g1[...] = mid.astype(BF16)
    for k, d in enumerate((2, 1, 3)):
        rows = pl.multiple_of(_rem(x + d, NX) * piece, 64)
        cp = remote(g1.at[pl.ds(rows, piece)], g1land.at[k], m_send.at[1 + k], m_recv.at[1 + k], device(dx=d))
        cp.start()
        sent.append(cp)
    own_rows = pl.multiple_of(x * piece, 64)
    for k in range(3):
        arrival(g1land.at[k], m_recv.at[1 + k]).wait_recv()
    low = gram[pl.ds(own_rows, piece), :]
    low = low + g1land[0].astype(F32) + g1land[1].astype(F32) + g1land[2].astype(F32)
    g2[...] = low.astype(BF16)
    cp = remote(g2, g2land, m_send.at[4], m_recv.at[4], device(dz=4))
    cp.start()
    sent.append(cp)
    cp.wait_recv()
    final_rows = pl.multiple_of(c * half_rows + x * piece, 64)
    final = gram_out.at[pl.ds(final_rows, piece)]
    gram_out[pl.ds(final_rows, piece), :] = (g2[...].astype(F32) + g2land[...].astype(F32)).astype(BF16)
    for k, d in enumerate((2, 1, 3)):
        cp = remote(final, final, m_send.at[5 + k], m_recv.at[5 + k], device(dx=d))
        cp.start()
        sent.append(cp)
    for k, d in enumerate((2, 1, 3)):
        rows = pl.multiple_of(c * half_rows + _rem(x - d, NX) * piece, 64)
        arrival(gram_out.at[pl.ds(rows, piece)], m_recv.at[5 + k]).wait_recv()
    mine_half = gram_out.at[pl.ds(pl.multiple_of(c * half_rows, 128), half_rows)]
    cp = remote(mine_half, mine_half, m_send.at[8], m_recv.at[8], device(dc=1))
    cp.start()
    sent.append(cp)
    arrival(gram_out.at[pl.ds(pl.multiple_of((1 - c) * half_rows, 128), half_rows)], m_recv.at[8]).wait_recv()

    for cp in sent:
        cp.wait_send()
    for j in range(n):
        g_drain(j)


def gradient_call(act, grad, blk):
    tok, ff = grad.shape
    n, wide = len(WIDTHS), max(WIDTHS)
    row, piece = blk // NX, blk // 2 // NX
    dma = pltpu.SemaphoreType.DMA
    flops = 2 * tok * NZ * blk * NY * ff + 2 * blk * blk * ff
    return pl.pallas_call(
        gradient_kernel,
        out_shape=(jax.ShapeDtypeStruct((blk, ff), BF16), jax.ShapeDtypeStruct((blk, blk), BF16)),
        in_specs=[pl.BlockSpec(memory_space=pl.ANY)] * 2,
        out_specs=[pl.BlockSpec(memory_space=pltpu.VMEM)] * 2,
        scratch_shapes=[
            pltpu.VMEM((6, tok, row), BF16),
            pltpu.VMEM((NY, tok, blk), BF16),
            pltpu.VMEM((6, row, tok), BF16),
            pltpu.VMEM((NY, blk, NZ * tok), BF16),
            pltpu.VMEM((n, NZ * tok, wide), BF16),
            pltpu.VMEM((n, NY - 1, blk, wide), BF16),
            pltpu.VMEM((n, NY - 1, blk, wide), BF16),
            pltpu.VMEM((2, blk, wide), F32),
            pltpu.VMEM((blk, blk), F32),
            pltpu.VMEM((blk, blk), BF16),
            pltpu.VMEM((blk // 2, blk), BF16),
            pltpu.VMEM((blk // 2, blk), BF16),
            pltpu.VMEM((3, piece, blk), BF16),
            pltpu.VMEM((piece, blk), BF16),
            pltpu.VMEM((piece, blk), BF16),
            dma((10 + n,)), dma((6,)), dma((6,)), dma((6, 3)), dma((6, 3)), dma((6,)), dma((6,)),
            dma((n, 5)), dma((n, 4)), dma((n, 3)), dma((n, 3)), dma((9,)), dma((9,)),
        ],
        compiler_params=pltpu.CompilerParams(
            collective_id=0, has_side_effects=True, vmem_limit_bytes=56 * 2**20
        ),
        cost_estimate=pl.CostEstimate(flops=flops, bytes_accessed=8 * 2**20, transcendentals=0),
        name="gradient",
    )(act, grad)


def _mm(a, b):
    return jnp.dot(a.astype(BF16), b.astype(BF16), preferred_element_type=F32)


def root_kernel(refresh, gram, left, old, red, stats, roots, update, state, root, square):
    blk = gram.shape[0]
    me = lax.axis_index("dp")
    new = STAT_DECAY * left[...] + (1.0 / FF) * gram[...].astype(F32)
    stats[...] = new
    picked = refresh[0] == me
    for i in range(1, refresh.shape[0]):
        picked = picked | (refresh[i] == me)

    @pl.when(picked)
    def _():
        value = stats[...]
        norm = blk * jnp.sqrt(jnp.mean(value * value, keepdims=True) + 1e-6)
        scale = jnp.exp(-0.25 * jnp.log(norm))
        state[...] = value * (0.25 / norm)
        eye = (
            lax.broadcasted_iota(jnp.int32, (blk, blk), 0) == lax.broadcasted_iota(jnp.int32, (blk, blk), 1)
        ).astype(F32)
        root[...] = scale * (1.25 * eye - state[...])
        for i in range(ITERS - 1):
            half = state[...].astype(BF16)
            square[...] = jnp.dot(half, half, preferred_element_type=F32)
            cube = jnp.dot(half, square[...].astype(BF16), preferred_element_type=F32)
            cube = 9.375 * state[...] - 5.0 * square[...] + cube
            last = _mm(square[...], cube)
            state[...] = 2.44140625 * state[...] - 7.8125 * square[...] + last
            root[...] = 1.25 * root[...] - _mm(root[...], state[...])
        roots[...] = root[...]

    @pl.when(jnp.logical_not(picked))
    def _():
        roots[...] = old[...]

    update[...] = jnp.dot(roots[...].astype(BF16), red[...], preferred_element_type=F32).astype(BF16)


def root_call(refresh, gram, left, old, red):
    blk, ff = red.shape
    vmem = pl.BlockSpec(memory_space=pltpu.VMEM)
    return pl.pallas_call(
        root_kernel,
        out_shape=(
            jax.ShapeDtypeStruct((blk, blk), F32),
            jax.ShapeDtypeStruct((blk, blk), F32),
            jax.ShapeDtypeStruct((blk, ff), BF16),
        ),
        in_specs=[pl.BlockSpec(memory_space=pltpu.SMEM)] + [vmem] * 4,
        out_specs=[vmem] * 3,
        scratch_shapes=[pltpu.VMEM((blk, blk), F32)] * 3,
        compiler_params=pltpu.CompilerParams(vmem_limit_bytes=40 * 2**20),
        name="root",
    )(refresh, gram, left, old, red)


def per_device(activations, out_grads, left_stats, old_roots, refresh):
    reduced, gram = gradient_call(activations, out_grads, left_stats.shape[1])
    return root_call(refresh, gram, left_stats, old_roots, reduced)


def solution(mesh):
    placed = (P("dp", None), P("dp", "tensor"), P("dp", None), P("dp", None), P())
    return jax.shard_map(
        per_device,
        mesh=mesh,
        in_specs=placed,
        out_specs=(P("dp", None), P("dp", None), P("dp", "tensor")),
        check_vma=False,
    )
```

```python
import functools

import jax
import jax.numpy as jnp
from jax import lax
from jax.experimental import pallas as pl
from jax.experimental.pallas import tpu as pltpu
from jax.sharding import PartitionSpec as P

FF = 16384
ITERS = 6
STAT_DECAY = 0.8
NZ, NY, NX, NC = 4, 4, 4, 2
MESH = pl.DeviceIdType.MESH
WIDTHS = (128, 128, 128, 128, 128, 128, 128, 128)
STARTS = tuple(sum(WIDTHS[:i]) for i in range(len(WIDTHS)))
Z_FIRST = (False, True, False, True, False, False, True, False)
DIRECT = ()
ORDER = (3, 2, 1, 0)
OWN, KEPT = len(WIDTHS), len(WIDTHS)
TILE = 128
PAIRS = tuple((i, j) for i in range(4) for j in range(i + 1))
BF16, F32 = jnp.bfloat16, jnp.float32


def _rem(a, n):
    return lax.rem(a + 2 * n, n)


def gradient_kernel(
    act, grad, red, gram_out,
    raw_near, raw_own, mine, at, gall, part, land, kept, own_part,
    gram, gram_half, gsend, gcore, g1, g1land, g2, g2land,
    load_sem, az_send, az_recv, ax_send, ax_recv, ac_send, ac_recv,
    g_send, g_recv, p_send, p_recv, m_send, m_recv,
):
    tok = act.shape[0]
    blk = red.shape[0]
    row = blk // NX
    share = row // NC
    dp, tn = lax.axis_index("dp"), lax.axis_index("tensor")
    zl, y = dp // NY, lax.rem(dp, NY)
    zh, x, c = tn // (NX * NC), lax.rem(tn // NC, NX), lax.rem(tn, NC)
    z = zh * NZ + zl

    def device(dz=0, dy=0, dx=0, dc=0):
        pz = _rem(z + dz, 2 * NZ)
        return (
            lax.rem(pz, NZ) * NY + _rem(y + dy, NY),
            (pz // NZ) * NX * NC + _rem(x + dx, NX) * NC + _rem(c + dc, NC),
        )

    def remote(src, dst, send, recv, to):
        return pltpu.make_async_remote_copy(
            src_ref=src, dst_ref=dst, send_sem=send, recv_sem=recv, device_id=to, device_id_type=MESH
        )

    def arrival(dst, recv):
        return remote(dst, dst, recv, recv, device(dc=1))

    far = jnp.where(c == 0, 2, -2)
    line = jnp.where(zl < 2, 2, -2)
    near = 1 - 2 * lax.rem(zl, 2)
    even_y = 1 - 2 * lax.rem(y, 2)
    back_y = NY - 1 - 2 * y

    def row_block(dz2, dy1, r):
        rz = _rem(zl + 2 * dz2, NZ)
        ry = y + even_y * dy1
        rz = rz + (1 - 2 * lax.rem(rz, 2)) * (r % 2)
        ry = ry + (NY - 1 - 2 * ry) * (r // 2)
        return rz * NY + ry

    sources = ((1, 0), (0, 1), (1, 1))
    near_load = {}
    for r in ORDER:
        for i, (dz2, dy1) in enumerate(sources):
            col = row_block(dz2, dy1, r) * blk + x * row
            cp = pltpu.make_async_copy(
                act.at[:, pl.ds(pl.multiple_of(col, 128), row)], raw_near.at[r * 3 + i], load_sem.at[r * 3 + i]
            )
            cp.start()
            near_load[r, i] = cp
    own_load = []
    for r in range(NY):
        col = row_block(0, 0, r) * blk
        cp = pltpu.make_async_copy(act.at[:, pl.ds(pl.multiple_of(col, 128), blk)], raw_own.at[r], load_sem.at[12 + r])
        cp.start()
        own_load.append(cp)
    g_load = []
    for j, (s, wd) in enumerate(zip(STARTS, WIDTHS)):
        cp = pltpu.make_async_copy(grad.at[:, pl.ds(s, wd)], gall.at[j, pl.ds(0, tok), pl.ds(0, wd)], load_sem.at[16 + j])
        cp.start()
        g_load.append(cp)

    barrier = pltpu.get_barrier_semaphore()
    peers = [device(dz=d) for d in (2, -2, 4)] + [device(dz=d, dy=even_y) for d in (2, -2)]
    peers += [device(dz=near), device(dy=even_y), device(dy=back_y), device(dz=near, dy=back_y)]
    peers += [device(dx=d) for d in (1, 2, 3)] + [device(dc=1)]
    for p in peers:
        pl.semaphore_signal(barrier, inc=1, device_id=p, device_id_type=MESH)
    pl.semaphore_wait(barrier, len(peers))

    sent = []

    def g_copy(j, src, dst, to):
        cols = pl.ds(0, WIDTHS[j])
        cp = remote(
            gall.at[j, pl.ds(src * tok, tok), cols], gall.at[j, pl.ds(dst * tok, tok), cols],
            g_send.at[j, dst], g_recv.at[j, dst], to,
        )
        cp.start()
        sent.append(cp)

    def g_own(j):
        g_load[j].wait()
        g_copy(j, 0, 1, device(dz=line))
        g_copy(j, 0, 2, device(dy=even_y))

    def g_wait(j, slot):
        arrival(gall.at[j, pl.ds(slot * tok, tok), pl.ds(0, WIDTHS[j])], g_recv.at[j, slot]).wait_recv()

    def g_pass(j):
        g_wait(j, 1)
        g_copy(j, 1, 3, device(dy=even_y))

    def g_rest(j):
        g_wait(j, 2)
        g_wait(j, 3)

    def columns(i):
        return pl.ds((i + 1) * tok, tok)

    def a_send(r):
        for i, (dz2, dy1) in enumerate(sources):
            near_load[r, i].wait()
            mine[r * 3 + i] = raw_near[r * 3 + i].T
            cp = remote(
                mine.at[r * 3 + i, pl.ds(pl.multiple_of(c * share, share), share)], at.at[r, x, c, :, columns(i)],
                az_send.at[r * 3 + i], az_recv.at[r * 3 + i], device(dz=far * dz2, dy=even_y * dy1),
            )
            cp.start()
            sent.append(cp)

    def a_share(r):
        for i in range(3):
            piece = at.at[r, x, c, :, columns(i)]
            arrival(piece, az_recv.at[r * 3 + i]).wait_recv()
            for k, d in enumerate((1, -1)):
                cp = remote(piece, piece, ax_send.at[r * 3 + i, k], ax_recv.at[r * 3 + i, k], device(dx=d))
                cp.start()
                sent.append(cp)

    def a_relay(r):
        for i in range(3):
            for k, d in enumerate((1, -1)):
                origin = _rem(x - d, NX)
                arrival(at.at[r, origin, c, :, columns(i)], ax_recv.at[r * 3 + i, k]).wait_recv()
                piece = at.at[r, origin, c, pl.ds(k * (share // 2), share // 2), columns(i)]
                cp = remote(piece, piece, ax_send.at[r * 3 + i, 2 + k], ax_recv.at[r * 3 + i, 2 + k], device(dx=d))
                cp.start()
                sent.append(cp)

    def a_core(r):
        origin = _rem(x + 2, NX)
        for i in range(3):
            for k in range(2):
                piece = at.at[r, origin, c, pl.ds(k * (share // 2), share // 2), columns(i)]
                arrival(piece, ax_recv.at[r * 3 + i, 2 + k]).wait_recv()
        piece = at.at[r, :, c, :, pl.ds(tok, 3 * tok)]
        cp = remote(piece, piece, ac_send.at[r], ac_recv.at[r], device(dc=1))
        cp.start()
        sent.append(cp)

    def a_wait(r):
        arrival(at.at[r, :, 1 - c, :, pl.ds(tok, 3 * tok)], ac_recv.at[r]).wait_recv()

    def first(j):
        return device(dz=near) if Z_FIRST[j] else device(dy=back_y)

    def second(j):
        return device(dy=back_y) if Z_FIRST[j] else device(dz=near)

    def p_copy(j, k, to):
        cols = pl.ds(0, WIDTHS[j])
        cp = remote(part.at[j, k, :, cols], land.at[j, k, :, cols], p_send.at[j, k], p_recv.at[j, k], to)
        cp.start()
        sent.append(cp)

    def p_wait(j, k):
        arrival(land.at[j, k, :, pl.ds(0, WIDTHS[j])], p_recv.at[j, k]).wait_recv()

    def product(j, r):
        wd = WIDTHS[j]
        value = jnp.dot(at[r].reshape(blk, NZ * tok), gall[j, :, 0:wd], preferred_element_type=F32)
        if j in DIRECT and r > 0:
            part[j, r - 1, :, 0:wd] = value.astype(BF16)
            p_copy(j, r - 1, device(dz=near * (r % 2), dy=back_y * (r // 2)))
        elif r == 0:
            own_part[j % OWN, :, 0:wd] = value
        elif r == (2 if Z_FIRST[j] else 1):
            kept[j % KEPT, :, 0:wd] = value
        else:
            k = 0 if r == 3 else 1
            part[j, k, :, 0:wd] = value.astype(BF16)
            p_copy(j, k, first(j))

    def p_pass(j):
        wd = WIDTHS[j]
        p_wait(j, 0)
        part[j, 2, :, 0:wd] = (kept[j % KEPT, :, 0:wd] + land[j, 0, :, 0:wd].astype(F32)).astype(BF16)
        p_copy(j, 2, second(j))

    def finish(j):
        wd = WIDTHS[j]
        p_wait(j, 1)
        p_wait(j, 2)
        total = own_part[j % OWN, :, 0:wd]
        if j in DIRECT:
            p_wait(j, 0)
            total = total + land[j, 0, :, 0:wd].astype(F32)
        total = total + land[j, 1, :, 0:wd].astype(F32) + land[j, 2, :, 0:wd].astype(F32)
        red[:, STARTS[j]:STARTS[j] + wd] = total.astype(BF16)
        half = red[:, STARTS[j]:STARTS[j] + wd]
        for i in range(blk // TILE):
            term = lax.dot_general(
                half[i * TILE:(i + 1) * TILE], half[:(i + 1) * TILE], (((1,), (1,)), ((), ())), preferred_element_type=F32
            )
            for k in range(i + 1):
                at_row = PAIRS.index((i, k)) * TILE
                tile = term[:, k * TILE:(k + 1) * TILE]
                if j == 0:
                    gram[at_row:at_row + TILE] = tile
                else:
                    gram[at_row:at_row + TILE] += tile

    def turn_own(r):
        own_load[r].wait()
        at[r, :, :, :, 0:tok] = raw_own[r].T.reshape(NX, NC, share, tok)

    n = len(WIDTHS)
    a_send(3)
    a_send(2)
    a_send(1)
    a_send(0)
    g_own(0)
    g_own(1)
    g_own(2)
    g_own(3)
    turn_own(3)
    turn_own(2)
    turn_own(1)
    turn_own(0)
    a_share(3)
    a_share(2)
    a_share(1)
    a_relay(3)
    a_share(0)
    a_relay(2)
    g_pass(0)
    g_own(4)
    a_relay(1)
    a_core(3)
    g_pass(1)
    g_own(5)
    g_rest(0)
    a_wait(3)
    product(0, 3)
    a_relay(0)
    g_pass(2)
    g_own(6)
    a_core(2)
    g_rest(1)
    product(1, 3)
    a_core(1)
    a_wait(2)
    product(0, 2)
    product(1, 2)
    a_core(0)
    g_pass(3)
    g_own(7)
    a_wait(1)
    product(0, 1)
    p_pass(0)
    product(1, 1)
    g_rest(2)
    product(2, 3)
    product(2, 2)
    product(2, 1)
    a_wait(0)
    product(0, 0)
    product(1, 0)
    p_pass(1)
    product(2, 0)
    g_pass(4)
    g_rest(3)
    product(3, 3)
    product(3, 1)
    product(3, 2)
    product(3, 0)
    p_pass(2)
    finish(0)
    g_pass(5)
    g_rest(4)
    product(4, 3)
    product(4, 2)
    product(4, 1)
    product(4, 0)
    finish(1)
    g_pass(6)
    g_rest(5)
    product(5, 3)
    product(5, 2)
    p_pass(3)
    product(5, 1)
    product(5, 0)
    p_pass(4)
    g_pass(7)
    g_rest(6)
    product(6, 3)
    product(6, 1)
    product(6, 2)
    product(6, 0)
    finish(2)
    p_pass(5)
    g_rest(7)
    product(7, 3)
    product(7, 2)
    product(7, 1)
    product(7, 0)
    finish(4)
    p_pass(6)
    finish(3)
    p_pass(7)
    finish(5)
    finish(7)
    finish(6)

    half_rows = gram.shape[0] // 2
    piece = half_rows // NX
    gsend[...] = gram[...].astype(BF16)
    other = remote(
        gsend.at[pl.ds(pl.multiple_of((1 - c) * half_rows, 128), half_rows)], gcore,
        m_send.at[0], m_recv.at[0], device(dc=1),
    )
    other.start()
    sent.append(other)
    other.wait_recv()
    mid = gram[pl.ds(pl.multiple_of(c * half_rows, 128), half_rows), :] + gcore[...].astype(F32)
    gram[0:half_rows, :] = mid
    g1[...] = mid.astype(BF16)
    for k, d in enumerate((2, 1, 3)):
        rows = pl.multiple_of(_rem(x + d, NX) * piece, 32)
        cp = remote(g1.at[pl.ds(rows, piece)], g1land.at[k], m_send.at[1 + k], m_recv.at[1 + k], device(dx=d))
        cp.start()
        sent.append(cp)
    own_rows = pl.multiple_of(x * piece, 32)
    for k in range(3):
        arrival(g1land.at[k], m_recv.at[1 + k]).wait_recv()
    low = gram[pl.ds(own_rows, piece), :]
    low = low + g1land[0].astype(F32) + g1land[1].astype(F32) + g1land[2].astype(F32)
    g2[...] = low.astype(BF16)
    cp = remote(g2, g2land, m_send.at[4], m_recv.at[4], device(dz=4))
    cp.start()
    sent.append(cp)
    cp.wait_recv()
    final_rows = pl.multiple_of(c * half_rows + x * piece, 32)
    final = gram_half.at[pl.ds(final_rows, piece)]
    gram_half[pl.ds(final_rows, piece), :] = (g2[...].astype(F32) + g2land[...].astype(F32)).astype(BF16)
    for k, d in enumerate((2, 1, 3)):
        cp = remote(final, final, m_send.at[5 + k], m_recv.at[5 + k], device(dx=d))
        cp.start()
        sent.append(cp)
    for k, d in enumerate((2, 1, 3)):
        rows = pl.multiple_of(c * half_rows + _rem(x - d, NX) * piece, 32)
        arrival(gram_half.at[pl.ds(rows, piece)], m_recv.at[5 + k]).wait_recv()
    mine_half = gram_half.at[pl.ds(pl.multiple_of(c * half_rows, 128), half_rows)]
    cp = remote(mine_half, mine_half, m_send.at[8], m_recv.at[8], device(dc=1))
    cp.start()
    sent.append(cp)
    arrival(gram_half.at[pl.ds(pl.multiple_of((1 - c) * half_rows, 128), half_rows)], m_recv.at[8]).wait_recv()

    gram_out[...] = gram_half[...]

    for cp in sent:
        cp.wait_send()


def gradient_call(act, grad, blk):
    tok, ff = grad.shape
    n, wide = len(WIDTHS), max(WIDTHS)
    row = blk // NX
    packed = len(PAIRS) * TILE
    dma = pltpu.SemaphoreType.DMA
    flops = 2 * tok * NZ * blk * NY * ff + 2 * blk * blk * ff
    return pl.pallas_call(
        gradient_kernel,
        out_shape=(pltpu.VMEM((blk, ff), BF16), pltpu.VMEM((packed, TILE), BF16)),
        in_specs=[pl.BlockSpec(memory_space=pl.ANY)] * 2,
        out_specs=[pl.BlockSpec(memory_space=pltpu.VMEM)] * 2,
        scratch_shapes=[
            pltpu.VMEM((12, tok, row), BF16),
            pltpu.VMEM((NY, tok, blk), BF16),
            pltpu.VMEM((12, row, tok), BF16),
            pltpu.VMEM((NY, NX, NC, row // NC, NZ * tok), BF16),
            pltpu.VMEM((n, NZ * tok, wide), BF16),
            pltpu.VMEM((n, 3, blk, wide), BF16),
            pltpu.VMEM((n, 3, blk, wide), BF16),
            pltpu.VMEM((KEPT, blk, wide), F32),
            pltpu.VMEM((OWN, blk, wide), F32),
            pltpu.VMEM((packed, TILE), F32),
            pltpu.VMEM((packed, TILE), BF16),
            pltpu.VMEM((packed, TILE), BF16),
            pltpu.VMEM((packed // 2, TILE), BF16),
            pltpu.VMEM((packed // 2, TILE), BF16),
            pltpu.VMEM((3, packed // 8, TILE), BF16),
            pltpu.VMEM((packed // 8, TILE), BF16),
            pltpu.VMEM((packed // 8, TILE), BF16),
            dma((16 + n,)), dma((12,)), dma((12,)), dma((12, 4)), dma((12, 4)), dma((NY,)), dma((NY,)),
            dma((n, 4)), dma((n, 4)), dma((n, 3)), dma((n, 3)), dma((9,)), dma((9,)),
        ],
        compiler_params=pltpu.CompilerParams(
            collective_id=0, has_side_effects=True, vmem_limit_bytes=56 * 2**20
        ),
        cost_estimate=pl.CostEstimate(flops=flops, bytes_accessed=8 * 2**20, transcendentals=0),
        name="gradient",
    )(act, grad)


def _mm(a, b):
    return jnp.dot(a.astype(BF16), b.astype(BF16), preferred_element_type=F32)


def root_kernel(refresh, gram, left, old, red, stats, roots, update, state, root, square):
    blk = left.shape[0]
    me = lax.axis_index("dp")
    for k, (i, j) in enumerate(PAIRS):
        term = (1.0 / FF) * gram[k * TILE:(k + 1) * TILE].astype(F32)
        rows, cols = slice(i * TILE, (i + 1) * TILE), slice(j * TILE, (j + 1) * TILE)
        stats[rows, cols] = STAT_DECAY * left[rows, cols] + term
        if i != j:
            stats[cols, rows] = STAT_DECAY * left[cols, rows] + term.T
    picked = refresh[0] == me
    for i in range(1, refresh.shape[0]):
        picked = picked | (refresh[i] == me)

    @pl.when(picked)
    def _():
        value = stats[...]
        norm = blk * jnp.sqrt(jnp.mean(value * value, keepdims=True) + 1e-6)
        scale = jnp.exp(-0.25 * jnp.log(norm))
        state[...] = value * (0.25 / norm)
        eye = (
            lax.broadcasted_iota(jnp.int32, (blk, blk), 0) == lax.broadcasted_iota(jnp.int32, (blk, blk), 1)
        ).astype(F32)
        root[...] = scale * (1.25 * eye - state[...])
        for i in range(ITERS - 1):
            half = state[...].astype(BF16)
            square[...] = jnp.dot(half, half, preferred_element_type=F32)
            cube = jnp.dot(half, square[...].astype(BF16), preferred_element_type=F32)
            cube = 9.375 * state[...] - 5.0 * square[...] + cube
            last = _mm(square[...], cube)
            state[...] = 2.44140625 * state[...] - 7.8125 * square[...] + last
            root[...] = 1.25 * root[...] - _mm(root[...], state[...])
        roots[...] = root[...]

    @pl.when(jnp.logical_not(picked))
    def _():
        roots[...] = old[...]

    update[...] = jnp.dot(roots[...].astype(BF16), red[...], preferred_element_type=F32).astype(BF16)


def root_call(refresh, gram, left, old, red):
    blk, ff = red.shape
    vmem = pl.BlockSpec(memory_space=pltpu.VMEM)
    return pl.pallas_call(
        root_kernel,
        out_shape=(
            jax.ShapeDtypeStruct((blk, blk), F32),
            jax.ShapeDtypeStruct((blk, blk), F32),
            jax.ShapeDtypeStruct((blk, ff), BF16),
        ),
        in_specs=[pl.BlockSpec(memory_space=pltpu.SMEM)] + [vmem] * 4,
        out_specs=[vmem] * 3,
        scratch_shapes=[pltpu.VMEM((blk, blk), F32)] * 3,
        compiler_params=pltpu.CompilerParams(vmem_limit_bytes=40 * 2**20),
        name="root",
    )(refresh, gram, left, old, red)


def per_device(activations, out_grads, left_stats, old_roots, refresh):
    reduced, gram = gradient_call(activations, out_grads, left_stats.shape[1])
    return root_call(refresh, gram, left_stats, old_roots, reduced)


def solution(mesh):
    placed = (P("dp", None), P("dp", "tensor"), P("dp", None), P("dp", None), P())
    return jax.shard_map(
        per_device,
        mesh=mesh,
        in_specs=placed,
        out_specs=(P("dp", None), P("dp", None), P("dp", "tensor")),
        check_vma=False,
    )
```

```python
import functools

import jax
import jax.numpy as jnp
from jax import lax
from jax.experimental import pallas as pl
from jax.experimental.pallas import tpu as pltpu
from jax.sharding import PartitionSpec as P

FF = 16384
ITERS = 6
STAT_DECAY = 0.8
NZ, NY, NX, NC = 4, 4, 4, 2
MESH = pl.DeviceIdType.MESH
WIDTHS = (128, 128, 128, 128, 128, 128, 128, 128)
STARTS = tuple(sum(WIDTHS[:i]) for i in range(len(WIDTHS)))
SPLIT = 384
X_DIRECT = ()
ORDER = (3, 2, 1, 0)
TILE = 128
PAIRS = tuple((i, j) for i in range(4) for j in range(i + 1))
BF16, F32 = jnp.bfloat16, jnp.float32


def _rem(a, n):
    return lax.rem(a + 2 * n, n)


def gradient_kernel(
    act, grad, red, gram_out,
    raw_near, raw_own, mine, at, gall, part, fwd, land, kept, own_part,
    gram, gram_half, gsend, gcore, g1, g1land, g2, g2land,
    load_sem, az_send, az_recv, ax_send, ax_recv, ac_send, ac_recv,
    g_send, g_recv, p_send, p_recv, m_send, m_recv,
):
    tok = act.shape[0]
    blk = red.shape[0]
    row = blk // NX
    share = row // NC
    dp, tn = lax.axis_index("dp"), lax.axis_index("tensor")
    zl, y = dp // NY, lax.rem(dp, NY)
    zh, x, c = tn // (NX * NC), lax.rem(tn // NC, NX), lax.rem(tn, NC)
    z = zh * NZ + zl

    def device(dz=0, dy=0, dx=0, dc=0):
        pz = _rem(z + dz, 2 * NZ)
        return (
            lax.rem(pz, NZ) * NY + _rem(y + dy, NY),
            (pz // NZ) * NX * NC + _rem(x + dx, NX) * NC + _rem(c + dc, NC),
        )

    def remote(src, dst, send, recv, to):
        return pltpu.make_async_remote_copy(
            src_ref=src, dst_ref=dst, send_sem=send, recv_sem=recv, device_id=to, device_id_type=MESH
        )

    def arrival(dst, recv):
        return remote(dst, dst, recv, recv, device(dc=1))

    far = jnp.where(c == 0, 2, -2)
    line = jnp.where(zl < 2, 2, -2)
    near = 1 - 2 * lax.rem(zl, 2)
    even_y = 1 - 2 * lax.rem(y, 2)
    back_y = NY - 1 - 2 * y

    def row_block(dz2, dy1, r):
        rz = _rem(zl + 2 * dz2, NZ)
        ry = y + even_y * dy1
        rz = rz + (1 - 2 * lax.rem(rz, 2)) * (r % 2)
        ry = ry + (NY - 1 - 2 * ry) * (r // 2)
        return rz * NY + ry

    sources = ((1, 0), (0, 1), (1, 1))
    near_load = {}
    for r in ORDER:
        for i, (dz2, dy1) in enumerate(sources):
            col = row_block(dz2, dy1, r) * blk + x * row
            cp = pltpu.make_async_copy(
                act.at[:, pl.ds(pl.multiple_of(col, 128), row)], raw_near.at[r * 3 + i], load_sem.at[r * 3 + i]
            )
            cp.start()
            near_load[r, i] = cp
    own_load = []
    for r in range(NY):
        col = row_block(0, 0, r) * blk
        cp = pltpu.make_async_copy(act.at[:, pl.ds(pl.multiple_of(col, 128), blk)], raw_own.at[r], load_sem.at[12 + r])
        cp.start()
        own_load.append(cp)
    g_load = []
    for j, (s, wd) in enumerate(zip(STARTS, WIDTHS)):
        cp = pltpu.make_async_copy(grad.at[:, pl.ds(s, wd)], gall.at[j, pl.ds(0, tok), pl.ds(0, wd)], load_sem.at[16 + j])
        cp.start()
        g_load.append(cp)

    barrier = pltpu.get_barrier_semaphore()
    peers = [device(dz=d) for d in (2, -2, 4)] + [device(dz=d, dy=even_y) for d in (2, -2)]
    peers += [device(dz=near), device(dy=even_y), device(dy=back_y)]
    peers += [device(dx=d) for d in (1, 2, 3)] + [device(dc=1)]
    for p in peers:
        pl.semaphore_signal(barrier, inc=1, device_id=p, device_id_type=MESH)
    pl.semaphore_wait(barrier, len(peers))

    sent = []

    def g_copy(j, src, dst, to):
        cols = pl.ds(0, WIDTHS[j])
        cp = remote(
            gall.at[j, pl.ds(src * tok, tok), cols], gall.at[j, pl.ds(dst * tok, tok), cols],
            g_send.at[j, dst], g_recv.at[j, dst], to,
        )
        cp.start()
        sent.append(cp)

    def g_own(j):
        g_load[j].wait()
        g_copy(j, 0, 1, device(dz=line))
        g_copy(j, 0, 2, device(dy=even_y))

    def g_wait(j, slot):
        arrival(gall.at[j, pl.ds(slot * tok, tok), pl.ds(0, WIDTHS[j])], g_recv.at[j, slot]).wait_recv()

    def g_pass(j):
        g_wait(j, 1)
        g_copy(j, 1, 3, device(dy=even_y))

    def g_rest(j):
        g_wait(j, 2)
        g_wait(j, 3)

    def columns(i):
        return pl.ds((i + 1) * tok, tok)

    def a_send(r):
        for i, (dz2, dy1) in enumerate(sources):
            near_load[r, i].wait()
            mine[r * 3 + i] = raw_near[r * 3 + i].T
            cp = remote(
                mine.at[r * 3 + i, pl.ds(pl.multiple_of(c * share, share), share)], at.at[r, x, c, :, columns(i)],
                az_send.at[r * 3 + i], az_recv.at[r * 3 + i], device(dz=far * dz2, dy=even_y * dy1),
            )
            cp.start()
            sent.append(cp)

    def a_share(r, i):
        piece = at.at[r, x, c, :, columns(i)]
        arrival(piece, az_recv.at[r * 3 + i]).wait_recv()
        for k, d in enumerate((1, -1, 2) if r in X_DIRECT else (1, -1)):
            cp = remote(piece, piece, ax_send.at[r * 3 + i, k], ax_recv.at[r * 3 + i, k], device(dx=d))
            cp.start()
            sent.append(cp)

    def a_relay(r, i):
        for k, d in enumerate((1, -1)):
            origin = _rem(x - d, NX)
            arrival(at.at[r, origin, c, :, columns(i)], ax_recv.at[r * 3 + i, k]).wait_recv()
            if r in X_DIRECT:
                continue
            piece = at.at[r, origin, c, pl.ds(k * (share // 2), share // 2), columns(i)]
            cp = remote(piece, piece, ax_send.at[r * 3 + i, 2 + k], ax_recv.at[r * 3 + i, 2 + k], device(dx=d))
            cp.start()
            sent.append(cp)

    def a_core(r):
        origin = _rem(x + 2, NX)
        for i in range(3):
            if r in X_DIRECT:
                arrival(at.at[r, origin, c, :, columns(i)], ax_recv.at[r * 3 + i, 2]).wait_recv()
                continue
            for k in range(2):
                piece = at.at[r, origin, c, pl.ds(k * (share // 2), share // 2), columns(i)]
                arrival(piece, ax_recv.at[r * 3 + i, 2 + k]).wait_recv()
        piece = at.at[r, :, c, :, pl.ds(tok, 3 * tok)]
        cp = remote(piece, piece, ac_send.at[r], ac_recv.at[r], device(dc=1))
        cp.start()
        sent.append(cp)

    def a_wait(r):
        arrival(at.at[r, :, 1 - c, :, pl.ds(tok, 3 * tok)], ac_recv.at[r]).wait_recv()

    top, low = pl.ds(0, SPLIT), pl.ds(SPLIT, blk - SPLIT)
    count = (SPLIT, blk - SPLIT)
    z_peer, y_peer = device(dz=near), device(dy=back_y)

    def p_copy(j, k, src, dst, to):
        cp = remote(src, dst, p_send.at[j, k], p_recv.at[j, k], to)
        cp.start()
        sent.append(cp)

    def product(j, r):
        cols = pl.ds(0, WIDTHS[j])
        value = jnp.dot(at[r].reshape(blk, NZ * tok), gall[j, :, cols], preferred_element_type=F32)
        if r == 0:
            own_part[j, :, cols] = value
        elif r == 3:
            part[j, 2, :, cols] = value.astype(BF16)
            p_copy(j, 0, part.at[j, 2, top, cols], fwd.at[j, 0, top, cols], y_peer)
            p_copy(j, 1, part.at[j, 2, low, cols], fwd.at[j, 1, pl.ds(0, blk - SPLIT), cols], z_peer)
        elif r == 2:
            part[j, 1, top, cols] = value[:SPLIT].astype(BF16)
            kept[j, 1, 0:blk - SPLIT, cols] = value[SPLIT:]
            p_copy(j, 2, part.at[j, 1, top, cols], land.at[j, 1, top, cols], y_peer)
        else:
            part[j, 0, low, cols] = value[SPLIT:].astype(BF16)
            kept[j, 0, top, cols] = value[:SPLIT]
            p_copy(j, 3, part.at[j, 0, low, cols], land.at[j, 0, low, cols], z_peer)

    def p_pass(j, k):
        cols = pl.ds(0, WIDTHS[j])
        rows, to = ((top, z_peer), (low, y_peer))[k]
        held = pl.ds(0, count[k])
        arrival(fwd.at[j, k, held, cols], p_recv.at[j, k]).wait_recv()
        part[j, k, rows, cols] = (kept[j, k, held, cols] + fwd[j, k, held, cols].astype(F32)).astype(BF16)
        p_copy(j, 4 + k, part.at[j, k, rows, cols], land.at[j, k, rows, cols], to)

    def finish(j):
        wd = WIDTHS[j]
        cols = pl.ds(0, wd)
        for k, side, rows in ((2, 1, top), (3, 0, low), (4, 0, top), (5, 1, low)):
            arrival(land.at[j, side, rows, cols], p_recv.at[j, k]).wait_recv()
        total = own_part[j, :, cols] + land[j, 0, :, cols].astype(F32) + land[j, 1, :, cols].astype(F32)
        red[:, STARTS[j]:STARTS[j] + wd] = total.astype(BF16)
        half = red[:, STARTS[j]:STARTS[j] + wd]
        for i in range(blk // TILE):
            term = lax.dot_general(
                half[i * TILE:(i + 1) * TILE], half[:(i + 1) * TILE], (((1,), (1,)), ((), ())), preferred_element_type=F32
            )
            for k in range(i + 1):
                at_row = PAIRS.index((i, k)) * TILE
                tile = term[:, k * TILE:(k + 1) * TILE]
                if j == 0:
                    gram[at_row:at_row + TILE] = tile
                else:
                    gram[at_row:at_row + TILE] += tile

    def turn_own(r):
        own_load[r].wait()
        at[r, :, :, :, 0:tok] = raw_own[r].T.reshape(NX, NC, share, tok)

    n = len(WIDTHS)
    a_send(3)
    a_send(2)
    a_send(1)
    a_send(0)
    g_own(0)
    g_own(1)
    turn_own(3)
    turn_own(2)
    turn_own(1)
    a_share(3, 1)
    turn_own(0)
    a_share(3, 0)
    a_share(2, 1)
    a_share(3, 2)
    a_share(2, 0)
    a_share(1, 1)
    a_relay(3, 1)
    a_share(2, 2)
    a_share(1, 0)
    a_relay(3, 0)
    a_relay(2, 1)
    a_share(1, 2)
    a_relay(3, 2)
    a_relay(2, 0)
    a_relay(1, 1)
    a_relay(2, 2)
    a_share(0, 0)
    a_share(0, 1)
    a_share(0, 2)
    a_relay(1, 0)
    g_pass(0)
    g_own(2)
    a_relay(1, 2)
    a_core(3)
    a_core(2)
    g_pass(1)
    g_own(3)
    a_relay(0, 0)
    g_rest(0)
    a_wait(3)
    product(0, 3)
    a_relay(0, 1)
    a_wait(2)
    product(0, 2)
    a_relay(0, 2)
    a_core(1)
    g_pass(2)
    g_own(4)
    g_rest(1)
    product(1, 3)
    product(1, 2)
    p_pass(0, 1)
    a_wait(1)
    product(0, 1)
    a_core(0)
    p_pass(0, 0)
    product(1, 1)
    g_pass(3)
    g_own(5)
    a_wait(0)
    product(0, 0)
    product(1, 0)
    g_rest(2)
    product(2, 3)
    product(2, 2)
    p_pass(1, 1)
    p_pass(1, 0)
    product(2, 1)
    product(2, 0)
    g_pass(4)
    g_own(6)
    finish(0)
    g_rest(3)
    product(3, 3)
    product(3, 2)
    product(3, 1)
    product(3, 0)
    p_pass(2, 0)
    p_pass(2, 1)
    g_pass(5)
    g_own(7)
    g_rest(4)
    product(4, 3)
    product(4, 2)
    product(4, 1)
    finish(1)
    product(4, 0)
    p_pass(3, 0)
    g_pass(6)
    p_pass(3, 1)
    g_rest(5)
    product(5, 3)
    product(5, 2)
    product(5, 1)
    product(5, 0)
    finish(2)
    p_pass(4, 0)
    g_pass(7)
    g_rest(6)
    product(6, 3)
    product(6, 2)
    p_pass(4, 1)
    product(6, 1)
    product(6, 0)
    p_pass(5, 0)
    finish(3)
    g_rest(7)
    product(7, 3)
    p_pass(5, 1)
    product(7, 2)
    product(7, 1)
    product(7, 0)
    p_pass(6, 0)
    p_pass(6, 1)
    finish(4)
    p_pass(7, 1)
    p_pass(7, 0)
    finish(5)
    finish(6)
    finish(7)

    half_rows = gram.shape[0] // 2
    piece = half_rows // NX
    gsend[...] = gram[...].astype(BF16)
    other = remote(
        gsend.at[pl.ds(pl.multiple_of((1 - c) * half_rows, 128), half_rows)], gcore,
        m_send.at[0], m_recv.at[0], device(dc=1),
    )
    other.start()
    sent.append(other)
    other.wait_recv()
    mid = gram[pl.ds(pl.multiple_of(c * half_rows, 128), half_rows), :] + gcore[...].astype(F32)
    gram[0:half_rows, :] = mid
    g1[...] = mid.astype(BF16)
    for k, d in enumerate((2, 1, 3)):
        rows = pl.multiple_of(_rem(x + d, NX) * piece, 32)
        cp = remote(g1.at[pl.ds(rows, piece)], g1land.at[k], m_send.at[1 + k], m_recv.at[1 + k], device(dx=d))
        cp.start()
        sent.append(cp)
    own_rows = pl.multiple_of(x * piece, 32)
    for k in range(3):
        arrival(g1land.at[k], m_recv.at[1 + k]).wait_recv()
    low = gram[pl.ds(own_rows, piece), :]
    low = low + g1land[0].astype(F32) + g1land[1].astype(F32) + g1land[2].astype(F32)
    g2[...] = low.astype(BF16)
    cp = remote(g2, g2land, m_send.at[4], m_recv.at[4], device(dz=4))
    cp.start()
    sent.append(cp)
    cp.wait_recv()
    final_rows = pl.multiple_of(c * half_rows + x * piece, 32)
    final = gram_half.at[pl.ds(final_rows, piece)]
    gram_half[pl.ds(final_rows, piece), :] = (g2[...].astype(F32) + g2land[...].astype(F32)).astype(BF16)
    for k, d in enumerate((2, 1, 3)):
        cp = remote(final, final, m_send.at[5 + k], m_recv.at[5 + k], device(dx=d))
        cp.start()
        sent.append(cp)
    for k, d in enumerate((2, 1, 3)):
        rows = pl.multiple_of(c * half_rows + _rem(x - d, NX) * piece, 32)
        arrival(gram_half.at[pl.ds(rows, piece)], m_recv.at[5 + k]).wait_recv()
    mine_half = gram_half.at[pl.ds(pl.multiple_of(c * half_rows, 128), half_rows)]
    cp = remote(mine_half, mine_half, m_send.at[8], m_recv.at[8], device(dc=1))
    cp.start()
    sent.append(cp)
    arrival(gram_half.at[pl.ds(pl.multiple_of((1 - c) * half_rows, 128), half_rows)], m_recv.at[8]).wait_recv()

    gram_out[...] = gram_half[...]

    for cp in sent:
        cp.wait_send()


def gradient_call(act, grad, blk):
    tok, ff = grad.shape
    n, wide = len(WIDTHS), max(WIDTHS)
    row = blk // NX
    packed = len(PAIRS) * TILE
    dma = pltpu.SemaphoreType.DMA
    flops = 2 * tok * NZ * blk * NY * ff + 2 * blk * blk * ff
    return pl.pallas_call(
        gradient_kernel,
        out_shape=(pltpu.VMEM((blk, ff), BF16), pltpu.VMEM((packed, TILE), BF16)),
        in_specs=[pl.BlockSpec(memory_space=pl.ANY)] * 2,
        out_specs=[pl.BlockSpec(memory_space=pltpu.VMEM)] * 2,
        scratch_shapes=[
            pltpu.VMEM((12, tok, row), BF16),
            pltpu.VMEM((NY, tok, blk), BF16),
            pltpu.VMEM((12, row, tok), BF16),
            pltpu.VMEM((NY, NX, NC, row // NC, NZ * tok), BF16),
            pltpu.VMEM((n, NZ * tok, wide), BF16),
            pltpu.VMEM((n, 3, blk, wide), BF16),
            pltpu.VMEM((n, 2, SPLIT, wide), BF16),
            pltpu.VMEM((n, 2, blk, wide), BF16),
            pltpu.VMEM((n, 2, SPLIT, wide), F32),
            pltpu.VMEM((n, blk, wide), F32),
            pltpu.VMEM((packed, TILE), F32),
            pltpu.VMEM((packed, TILE), BF16),
            pltpu.VMEM((packed, TILE), BF16),
            pltpu.VMEM((packed // 2, TILE), BF16),
            pltpu.VMEM((packed // 2, TILE), BF16),
            pltpu.VMEM((3, packed // 8, TILE), BF16),
            pltpu.VMEM((packed // 8, TILE), BF16),
            pltpu.VMEM((packed // 8, TILE), BF16),
            dma((16 + n,)), dma((12,)), dma((12,)), dma((12, 4)), dma((12, 4)), dma((NY,)), dma((NY,)),
            dma((n, 4)), dma((n, 4)), dma((n, 6)), dma((n, 6)), dma((9,)), dma((9,)),
        ],
        compiler_params=pltpu.CompilerParams(
            collective_id=0, has_side_effects=True, vmem_limit_bytes=56 * 2**20
        ),
        cost_estimate=pl.CostEstimate(flops=flops, bytes_accessed=8 * 2**20, transcendentals=0),
        name="gradient",
    )(act, grad)


def _mm(a, b):
    return jnp.dot(a.astype(BF16), b.astype(BF16), preferred_element_type=F32)


def root_kernel(refresh, gram, left, old, red, stats, roots, update, state, root, square, pair):
    blk = left.shape[0]
    me = lax.axis_index("dp")
    for k, (i, j) in enumerate(PAIRS):
        term = (1.0 / FF) * gram[k * TILE:(k + 1) * TILE].astype(F32)
        rows, cols = slice(i * TILE, (i + 1) * TILE), slice(j * TILE, (j + 1) * TILE)
        stats[rows, cols] = STAT_DECAY * left[rows, cols] + term
        if i != j:
            stats[cols, rows] = STAT_DECAY * left[cols, rows] + term.T
    picked = refresh[0] == me
    for i in range(1, refresh.shape[0]):
        picked = picked | (refresh[i] == me)

    @pl.when(picked)
    def _():
        value = stats[...]
        norm = blk * jnp.sqrt(jnp.mean(value * value, keepdims=True) + 1e-6)
        scale = jnp.exp(-0.25 * jnp.log(norm))
        state[...] = value * (0.25 / norm)
        eye = (
            lax.broadcasted_iota(jnp.int32, (blk, blk), 0) == lax.broadcasted_iota(jnp.int32, (blk, blk), 1)
        ).astype(F32)
        root[...] = scale * (1.25 * eye - state[...])
        pair[0:blk] = state[...].astype(BF16)
        for i in range(ITERS - 1):
            half = pair[0:blk]
            if i == 0:
                square[...] = jnp.dot(half, half, preferred_element_type=F32)
            else:
                pair[blk:] = root[...].astype(BF16)
                both = jnp.dot(pair[...], half, preferred_element_type=F32)
                square[...] = both[0:blk]
                root[...] = 1.25 * root[...] - both[blk:]
            cube = jnp.dot(half, square[...].astype(BF16), preferred_element_type=F32)
            cube = 9.375 * state[...] - 5.0 * square[...] + cube
            last = _mm(square[...], cube)
            value = 2.44140625 * state[...] - 7.8125 * square[...] + last
            state[...] = value
            pair[0:blk] = value.astype(BF16)
        root[...] = 1.25 * root[...] - _mm(root[...], pair[0:blk])
        roots[...] = root[...]

    @pl.when(jnp.logical_not(picked))
    def _():
        roots[...] = old[...]

    update[...] = jnp.dot(roots[...].astype(BF16), red[...], preferred_element_type=F32).astype(BF16)


def root_call(refresh, gram, left, old, red):
    blk, ff = red.shape
    vmem = pl.BlockSpec(memory_space=pltpu.VMEM)
    return pl.pallas_call(
        root_kernel,
        out_shape=(
            jax.ShapeDtypeStruct((blk, blk), F32),
            jax.ShapeDtypeStruct((blk, blk), F32),
            jax.ShapeDtypeStruct((blk, ff), BF16),
        ),
        in_specs=[pl.BlockSpec(memory_space=pltpu.SMEM)] + [vmem] * 4,
        out_specs=[vmem] * 3,
        scratch_shapes=[pltpu.VMEM((blk, blk), F32)] * 3 + [pltpu.VMEM((2 * blk, blk), BF16)],
        compiler_params=pltpu.CompilerParams(vmem_limit_bytes=40 * 2**20),
        name="root",
    )(refresh, gram, left, old, red)


def per_device(activations, out_grads, left_stats, old_roots, refresh):
    reduced, gram = gradient_call(activations, out_grads, left_stats.shape[1])
    return root_call(refresh, gram, left_stats, old_roots, reduced)


def solution(mesh):
    placed = (P("dp", None), P("dp", "tensor"), P("dp", None), P("dp", None), P())
    return jax.shard_map(
        per_device,
        mesh=mesh,
        in_specs=placed,
        out_specs=(P("dp", None), P("dp", None), P("dp", "tensor")),
        check_vma=False,
    )
```

```python
import functools

import jax
import jax.numpy as jnp
from jax import lax
from jax.experimental import pallas as pl
from jax.experimental.pallas import tpu as pltpu
from jax.sharding import PartitionSpec as P

FF = 16384
ITERS = 6
STAT_DECAY = 0.8
NZ, NY, NX, NC = 4, 4, 4, 2
MESH = pl.DeviceIdType.MESH
WIDTHS = (128, 128, 128, 128, 128, 128, 128, 128)
STARTS = tuple(sum(WIDTHS[:i]) for i in range(len(WIDTHS)))
SPLIT = (384, 384, 384, 384, 384, 256, 256, 256)
X_DIRECT = ()
ORDER = (3, 2, 1, 0)
TILE = 128
PAIRS = tuple((i, j) for i in range(4) for j in range(i + 1))
BF16, F32 = jnp.bfloat16, jnp.float32


def _rem(a, n):
    return lax.rem(a + 2 * n, n)


def gradient_kernel(
    act, grad, red, gram_out,
    raw_near, raw_own, mine, at, gall, part, fwd, land, kept, own_part,
    gram, gram_half, gsend, gcore, g1, g1land, g2, g2land,
    load_sem, az_send, az_recv, ax_send, ax_recv, ac_send, ac_recv,
    g_send, g_recv, p_send, p_recv, m_send, m_recv,
):
    tok = act.shape[0]
    blk = red.shape[0]
    row = blk // NX
    share = row // NC
    dp, tn = lax.axis_index("dp"), lax.axis_index("tensor")
    zl, y = dp // NY, lax.rem(dp, NY)
    zh, x, c = tn // (NX * NC), lax.rem(tn // NC, NX), lax.rem(tn, NC)
    z = zh * NZ + zl

    def device(dz=0, dy=0, dx=0, dc=0):
        pz = _rem(z + dz, 2 * NZ)
        return (
            lax.rem(pz, NZ) * NY + _rem(y + dy, NY),
            (pz // NZ) * NX * NC + _rem(x + dx, NX) * NC + _rem(c + dc, NC),
        )

    def remote(src, dst, send, recv, to):
        return pltpu.make_async_remote_copy(
            src_ref=src, dst_ref=dst, send_sem=send, recv_sem=recv, device_id=to, device_id_type=MESH
        )

    def arrival(dst, recv):
        return remote(dst, dst, recv, recv, device(dc=1))

    line = jnp.where(zl < 2, 2, -2)
    far = -line
    near = 1 - 2 * lax.rem(zl, 2)
    even_y = 1 - 2 * lax.rem(y, 2)
    back_y = NY - 1 - 2 * y

    def row_block(dz2, dy1, r):
        rz = _rem(zl + 2 * dz2, NZ)
        ry = y + even_y * dy1
        rz = rz + (1 - 2 * lax.rem(rz, 2)) * (r % 2)
        ry = ry + (NY - 1 - 2 * ry) * (r // 2)
        return rz * NY + ry

    sources = ((1, 0), (0, 1), (1, 1))
    near_load = {}
    for r in ORDER:
        for i, (dz2, dy1) in enumerate(sources):
            col = row_block(dz2, dy1, r) * blk + x * row
            cp = pltpu.make_async_copy(
                act.at[:, pl.ds(pl.multiple_of(col, 128), row)], raw_near.at[r * 3 + i], load_sem.at[r * 3 + i]
            )
            cp.start()
            near_load[r, i] = cp
    own_load = []
    for r in range(NY):
        col = row_block(0, 0, r) * blk
        cp = pltpu.make_async_copy(act.at[:, pl.ds(pl.multiple_of(col, 128), blk)], raw_own.at[r], load_sem.at[12 + r])
        cp.start()
        own_load.append(cp)
    g_load = []
    for j, (s, wd) in enumerate(zip(STARTS, WIDTHS)):
        cp = pltpu.make_async_copy(grad.at[:, pl.ds(s, wd)], gall.at[j, pl.ds(0, tok), pl.ds(0, wd)], load_sem.at[16 + j])
        cp.start()
        g_load.append(cp)

    barrier = pltpu.get_barrier_semaphore()
    peers = [device(dz=d) for d in (2, -2, 4)] + [device(dz=d, dy=even_y) for d in (2, -2)]
    peers += [device(dz=near), device(dy=even_y), device(dy=back_y)]
    peers += [device(dx=d) for d in (1, 2, 3)] + [device(dc=1)]
    for p in peers:
        pl.semaphore_signal(barrier, inc=1, device_id=p, device_id_type=MESH)
    pl.semaphore_wait(barrier, len(peers))

    sent = []

    def g_copy(j, src, dst, to):
        cols = pl.ds(0, WIDTHS[j])
        cp = remote(
            gall.at[j, pl.ds(src * tok, tok), cols], gall.at[j, pl.ds(dst * tok, tok), cols],
            g_send.at[j, dst], g_recv.at[j, dst], to,
        )
        cp.start()
        sent.append(cp)

    def g_own(j):
        g_load[j].wait()
        g_copy(j, 0, 1, device(dz=line))
        g_copy(j, 0, 2, device(dy=even_y))

    def g_wait(j, slot):
        arrival(gall.at[j, pl.ds(slot * tok, tok), pl.ds(0, WIDTHS[j])], g_recv.at[j, slot]).wait_recv()

    def g_pass(j):
        g_wait(j, 1)
        g_copy(j, 1, 3, device(dy=even_y))

    def g_rest(j):
        g_wait(j, 2)
        g_wait(j, 3)

    def columns(i):
        return pl.ds((i + 1) * tok, tok)

    def a_send(r):
        for i, (dz2, dy1) in enumerate(sources):
            near_load[r, i].wait()
            mine[r * 3 + i] = raw_near[r * 3 + i].T
            cp = remote(
                mine.at[r * 3 + i, pl.ds(pl.multiple_of(c * share, share), share)], at.at[r, x, c, :, columns(i)],
                az_send.at[r * 3 + i], az_recv.at[r * 3 + i], device(dz=far * dz2, dy=even_y * dy1),
            )
            cp.start()
            sent.append(cp)

    def a_share(r, i):
        piece = at.at[r, x, c, :, columns(i)]
        arrival(piece, az_recv.at[r * 3 + i]).wait_recv()
        for k, d in enumerate((1, -1, 2) if r in X_DIRECT else (1, -1)):
            cp = remote(piece, piece, ax_send.at[r * 3 + i, k], ax_recv.at[r * 3 + i, k], device(dx=d))
            cp.start()
            sent.append(cp)

    def a_relay(r, i):
        for k, d in enumerate((1, -1)):
            origin = _rem(x - d, NX)
            arrival(at.at[r, origin, c, :, columns(i)], ax_recv.at[r * 3 + i, k]).wait_recv()
            if r in X_DIRECT:
                continue
            piece = at.at[r, origin, c, pl.ds(k * (share // 2), share // 2), columns(i)]
            cp = remote(piece, piece, ax_send.at[r * 3 + i, 2 + k], ax_recv.at[r * 3 + i, 2 + k], device(dx=d))
            cp.start()
            sent.append(cp)

    def a_core(r):
        origin = _rem(x + 2, NX)
        for i in range(3):
            if r in X_DIRECT:
                arrival(at.at[r, origin, c, :, columns(i)], ax_recv.at[r * 3 + i, 2]).wait_recv()
                continue
            for k in range(2):
                piece = at.at[r, origin, c, pl.ds(k * (share // 2), share // 2), columns(i)]
                arrival(piece, ax_recv.at[r * 3 + i, 2 + k]).wait_recv()
        piece = at.at[r, :, c, :, pl.ds(tok, 3 * tok)]
        cp = remote(piece, piece, ac_send.at[r], ac_recv.at[r], device(dc=1))
        cp.start()
        sent.append(cp)

    def a_wait(r):
        arrival(at.at[r, :, 1 - c, :, pl.ds(tok, 3 * tok)], ac_recv.at[r]).wait_recv()

    z_peer, y_peer = device(dz=near), device(dy=back_y)

    def p_copy(j, k, src, dst, to):
        cp = remote(src, dst, p_send.at[j, k], p_recv.at[j, k], to)
        cp.start()
        sent.append(cp)

    def parts(j):
        return pl.ds(0, SPLIT[j]), pl.ds(SPLIT[j], blk - SPLIT[j])

    def product(j, r):
        cols = pl.ds(0, WIDTHS[j])
        (top, low), cut = parts(j), SPLIT[j]
        value = jnp.dot(at[r].reshape(blk, NZ * tok), gall[j, :, cols], preferred_element_type=F32)
        if r == 0:
            own_part[j, :, cols] = value
        elif r == 3:
            part[j, 2, :, cols] = value.astype(BF16)
            p_copy(j, 0, part.at[j, 2, top, cols], fwd.at[j, 0, top, cols], y_peer)
            p_copy(j, 1, part.at[j, 2, low, cols], fwd.at[j, 1, pl.ds(0, blk - cut), cols], z_peer)
        elif r == 2:
            part[j, 1, top, cols] = value[:cut].astype(BF16)
            kept[j, 1, 0:blk - cut, cols] = value[cut:]
            p_copy(j, 2, part.at[j, 1, top, cols], land.at[j, 1, top, cols], y_peer)
        else:
            part[j, 0, low, cols] = value[cut:].astype(BF16)
            kept[j, 0, top, cols] = value[:cut]
            p_copy(j, 3, part.at[j, 0, low, cols], land.at[j, 0, low, cols], z_peer)

    def p_pass(j, k):
        cols = pl.ds(0, WIDTHS[j])
        rows, to = (parts(j)[k], (z_peer, y_peer)[k])
        held = pl.ds(0, (SPLIT[j], blk - SPLIT[j])[k])
        arrival(fwd.at[j, k, held, cols], p_recv.at[j, k]).wait_recv()
        part[j, k, rows, cols] = (kept[j, k, held, cols] + fwd[j, k, held, cols].astype(F32)).astype(BF16)
        p_copy(j, 4 + k, part.at[j, k, rows, cols], land.at[j, k, rows, cols], to)

    def finish(j):
        wd = WIDTHS[j]
        cols = pl.ds(0, wd)
        top, low = parts(j)
        for k, side, rows in ((2, 1, top), (3, 0, low), (4, 0, top), (5, 1, low)):
            arrival(land.at[j, side, rows, cols], p_recv.at[j, k]).wait_recv()
        total = own_part[j, :, cols] + land[j, 0, :, cols].astype(F32) + land[j, 1, :, cols].astype(F32)
        red[:, STARTS[j]:STARTS[j] + wd] = total.astype(BF16)
        half = red[:, STARTS[j]:STARTS[j] + wd]
        for i in range(blk // TILE):
            term = lax.dot_general(
                half[i * TILE:(i + 1) * TILE], half[:(i + 1) * TILE], (((1,), (1,)), ((), ())), preferred_element_type=F32
            )
            for k in range(i + 1):
                at_row = PAIRS.index((i, k)) * TILE
                tile = term[:, k * TILE:(k + 1) * TILE]
                if j == 0:
                    gram[at_row:at_row + TILE] = tile
                else:
                    gram[at_row:at_row + TILE] += tile

    def turn_own(r):
        own_load[r].wait()
        at[r, :, :, :, 0:tok] = raw_own[r].T.reshape(NX, NC, share, tok)

    n = len(WIDTHS)
    g_own(0)
    g_own(1)
    a_send(3)
    a_send(2)
    a_send(1)
    turn_own(3)
    turn_own(2)
    turn_own(1)
    turn_own(0)
    a_share(3, 0)
    a_share(3, 1)
    g_pass(0)
    g_own(2)
    a_share(3, 2)
    a_relay(3, 0)
    a_share(2, 1)
    a_share(2, 0)
    a_relay(3, 1)
    g_pass(1)
    g_own(3)
    a_share(2, 2)
    a_relay(3, 2)
    a_share(1, 1)
    a_share(1, 0)
    a_relay(2, 1)
    g_pass(2)
    g_own(4)
    a_relay(2, 0)
    a_share(1, 2)
    a_relay(2, 2)
    a_core(3)
    a_relay(1, 1)
    g_pass(3)
    g_own(5)
    a_send(0)
    a_relay(1, 0)
    g_rest(0)
    a_wait(3)
    product(0, 3)
    g_rest(1)
    product(1, 3)
    a_relay(1, 2)
    a_core(2)
    g_pass(4)
    g_own(6)
    a_wait(2)
    product(0, 2)
    a_core(1)
    product(1, 2)
    g_rest(2)
    product(2, 3)
    a_share(0, 0)
    product(2, 2)
    p_pass(0, 1)
    a_wait(1)
    product(0, 1)
    g_pass(5)
    g_own(7)
    product(1, 1)
    product(2, 1)
    p_pass(0, 0)
    p_pass(1, 0)
    p_pass(1, 1)
    g_rest(3)
    product(3, 3)
    a_relay(0, 0)
    p_pass(2, 1)
    product(3, 1)
    product(3, 2)
    g_pass(6)
    a_share(0, 1)
    p_pass(2, 0)
    a_share(0, 2)
    g_rest(4)
    product(4, 3)
    g_pass(7)
    a_relay(0, 1)
    product(4, 1)
    product(4, 2)
    a_relay(0, 2)
    p_pass(3, 0)
    p_pass(3, 1)
    g_rest(5)
    product(5, 3)
    product(5, 1)
    product(5, 2)
    a_core(0)
    p_pass(4, 1)
    p_pass(4, 0)
    g_rest(6)
    product(6, 3)
    product(6, 1)
    product(6, 2)
    a_wait(0)
    product(0, 0)
    product(1, 0)
    g_rest(7)
    product(7, 3)
    product(7, 1)
    p_pass(5, 1)
    product(7, 2)
    product(2, 0)
    product(3, 0)
    p_pass(5, 0)
    product(4, 0)
    finish(0)
    product(5, 0)
    finish(1)
    product(6, 0)
    finish(2)
    product(7, 0)
    finish(3)
    finish(4)
    p_pass(6, 0)
    p_pass(6, 1)
    p_pass(7, 0)
    p_pass(7, 1)
    finish(5)
    finish(6)
    finish(7)

    half_rows = gram.shape[0] // 2
    piece = half_rows // NX
    gsend[...] = gram[...].astype(BF16)
    other = remote(
        gsend.at[pl.ds(pl.multiple_of((1 - c) * half_rows, 128), half_rows)], gcore,
        m_send.at[0], m_recv.at[0], device(dc=1),
    )
    other.start()
    sent.append(other)
    other.wait_recv()
    mid = gram[pl.ds(pl.multiple_of(c * half_rows, 128), half_rows), :] + gcore[...].astype(F32)
    gram[0:half_rows, :] = mid
    g1[...] = mid.astype(BF16)
    for k, d in enumerate((2, 1, 3)):
        rows = pl.multiple_of(_rem(x + d, NX) * piece, 32)
        cp = remote(g1.at[pl.ds(rows, piece)], g1land.at[k], m_send.at[1 + k], m_recv.at[1 + k], device(dx=d))
        cp.start()
        sent.append(cp)
    own_rows = pl.multiple_of(x * piece, 32)
    for k in range(3):
        arrival(g1land.at[k], m_recv.at[1 + k]).wait_recv()
    low = gram[pl.ds(own_rows, piece), :]
    low = low + g1land[0].astype(F32) + g1land[1].astype(F32) + g1land[2].astype(F32)
    g2[...] = low.astype(BF16)
    cp = remote(g2, g2land, m_send.at[4], m_recv.at[4], device(dz=4))
    cp.start()
    sent.append(cp)
    cp.wait_recv()
    final_rows = pl.multiple_of(c * half_rows + x * piece, 32)
    final = gram_half.at[pl.ds(final_rows, piece)]
    gram_half[pl.ds(final_rows, piece), :] = (g2[...].astype(F32) + g2land[...].astype(F32)).astype(BF16)
    for k, d in enumerate((2, 1, 3)):
        cp = remote(final, final, m_send.at[5 + k], m_recv.at[5 + k], device(dx=d))
        cp.start()
        sent.append(cp)
    for k, d in enumerate((2, 1, 3)):
        rows = pl.multiple_of(c * half_rows + _rem(x - d, NX) * piece, 32)
        arrival(gram_half.at[pl.ds(rows, piece)], m_recv.at[5 + k]).wait_recv()
    mine_half = gram_half.at[pl.ds(pl.multiple_of(c * half_rows, 128), half_rows)]
    cp = remote(mine_half, mine_half, m_send.at[8], m_recv.at[8], device(dc=1))
    cp.start()
    sent.append(cp)
    arrival(gram_half.at[pl.ds(pl.multiple_of((1 - c) * half_rows, 128), half_rows)], m_recv.at[8]).wait_recv()

    gram_out[...] = gram_half[...]

    for cp in sent:
        cp.wait_send()


def gradient_call(act, grad, blk):
    tok, ff = grad.shape
    n, wide = len(WIDTHS), max(WIDTHS)
    row = blk // NX
    packed = len(PAIRS) * TILE
    dma = pltpu.SemaphoreType.DMA
    flops = 2 * tok * NZ * blk * NY * ff + 2 * blk * blk * ff
    return pl.pallas_call(
        gradient_kernel,
        out_shape=(pltpu.VMEM((blk, ff), BF16), pltpu.VMEM((packed, TILE), BF16)),
        in_specs=[pl.BlockSpec(memory_space=pl.ANY)] * 2,
        out_specs=[pl.BlockSpec(memory_space=pltpu.VMEM)] * 2,
        scratch_shapes=[
            pltpu.VMEM((12, tok, row), BF16),
            pltpu.VMEM((NY, tok, blk), BF16),
            pltpu.VMEM((12, row, tok), BF16),
            pltpu.VMEM((NY, NX, NC, row // NC, NZ * tok), BF16),
            pltpu.VMEM((n, NZ * tok, wide), BF16),
            pltpu.VMEM((n, 3, blk, wide), BF16),
            pltpu.VMEM((n, 2, max(SPLIT), wide), BF16),
            pltpu.VMEM((n, 2, blk, wide), BF16),
            pltpu.VMEM((n, 2, max(SPLIT), wide), F32),
            pltpu.VMEM((n, blk, wide), F32),
            pltpu.VMEM((packed, TILE), F32),
            pltpu.VMEM((packed, TILE), BF16),
            pltpu.VMEM((packed, TILE), BF16),
            pltpu.VMEM((packed // 2, TILE), BF16),
            pltpu.VMEM((packed // 2, TILE), BF16),
            pltpu.VMEM((3, packed // 8, TILE), BF16),
            pltpu.VMEM((packed // 8, TILE), BF16),
            pltpu.VMEM((packed // 8, TILE), BF16),
            dma((16 + n,)), dma((12,)), dma((12,)), dma((12, 4)), dma((12, 4)), dma((NY,)), dma((NY,)),
            dma((n, 4)), dma((n, 4)), dma((n, 6)), dma((n, 6)), dma((9,)), dma((9,)),
        ],
        compiler_params=pltpu.CompilerParams(
            collective_id=0, has_side_effects=True, vmem_limit_bytes=56 * 2**20
        ),
        cost_estimate=pl.CostEstimate(flops=flops, bytes_accessed=8 * 2**20, transcendentals=0),
        name="gradient",
    )(act, grad)


def _mm(a, b):
    return jnp.dot(a.astype(BF16), b.astype(BF16), preferred_element_type=F32)


def root_kernel(refresh, gram, left, old, red, stats, roots, update, state, root, square, pair):
    blk = left.shape[0]
    me = lax.axis_index("dp")
    for k, (i, j) in enumerate(PAIRS):
        term = (1.0 / FF) * gram[k * TILE:(k + 1) * TILE].astype(F32)
        rows, cols = slice(i * TILE, (i + 1) * TILE), slice(j * TILE, (j + 1) * TILE)
        stats[rows, cols] = STAT_DECAY * left[rows, cols] + term
        if i != j:
            stats[cols, rows] = STAT_DECAY * left[cols, rows] + term.T
    picked = refresh[0] == me
    for i in range(1, refresh.shape[0]):
        picked = picked | (refresh[i] == me)

    @pl.when(picked)
    def _():
        value = stats[...]
        norm = blk * jnp.sqrt(jnp.mean(value * value, keepdims=True) + 1e-6)
        scale = jnp.exp(-0.25 * jnp.log(norm))
        state[...] = value * (0.25 / norm)
        eye = (
            lax.broadcasted_iota(jnp.int32, (blk, blk), 0) == lax.broadcasted_iota(jnp.int32, (blk, blk), 1)
        ).astype(F32)
        root[...] = scale * (1.25 * eye - state[...])
        pair[0:blk] = state[...].astype(BF16)
        for i in range(ITERS - 1):
            half = pair[0:blk]
            if i == 0:
                square[...] = jnp.dot(half, half, preferred_element_type=F32)
            else:
                pair[blk:] = root[...].astype(BF16)
                both = jnp.dot(pair[...], half, preferred_element_type=F32)
                square[...] = both[0:blk]
                root[...] = 1.25 * root[...] - both[blk:]
            cube = jnp.dot(half, square[...].astype(BF16), preferred_element_type=F32)
            cube = 9.375 * state[...] - 5.0 * square[...] + cube
            last = _mm(square[...], cube)
            value = 2.44140625 * state[...] - 7.8125 * square[...] + last
            state[...] = value
            pair[0:blk] = value.astype(BF16)
        root[...] = 1.25 * root[...] - _mm(root[...], pair[0:blk])
        roots[...] = root[...]

    @pl.when(jnp.logical_not(picked))
    def _():
        roots[...] = old[...]

    update[...] = jnp.dot(roots[...].astype(BF16), red[...], preferred_element_type=F32).astype(BF16)


def root_call(refresh, gram, left, old, red):
    blk, ff = red.shape
    vmem = pl.BlockSpec(memory_space=pltpu.VMEM)
    return pl.pallas_call(
        root_kernel,
        out_shape=(
            jax.ShapeDtypeStruct((blk, blk), F32),
            jax.ShapeDtypeStruct((blk, blk), F32),
            jax.ShapeDtypeStruct((blk, ff), BF16),
        ),
        in_specs=[pl.BlockSpec(memory_space=pltpu.SMEM)] + [vmem] * 4,
        out_specs=[vmem] * 3,
        scratch_shapes=[pltpu.VMEM((blk, blk), F32)] * 3 + [pltpu.VMEM((2 * blk, blk), BF16)],
        compiler_params=pltpu.CompilerParams(vmem_limit_bytes=40 * 2**20),
        name="root",
    )(refresh, gram, left, old, red)


def per_device(activations, out_grads, left_stats, old_roots, refresh):
    reduced, gram = gradient_call(activations, out_grads, left_stats.shape[1])
    return root_call(refresh, gram, left_stats, old_roots, reduced)


def solution(mesh):
    placed = (P("dp", None), P("dp", "tensor"), P("dp", None), P("dp", None), P())
    return jax.shard_map(
        per_device,
        mesh=mesh,
        in_specs=placed,
        out_specs=(P("dp", None), P("dp", None), P("dp", "tensor")),
        check_vma=False,
    )
```

```python
import functools

import jax
import jax.numpy as jnp
from jax import lax
from jax.experimental import pallas as pl
from jax.experimental.pallas import tpu as pltpu
from jax.sharding import PartitionSpec as P

FF = 16384
ITERS = 6
STAT_DECAY = 0.8
NZ, NY, NX, NC = 4, 4, 4, 2
MESH = pl.DeviceIdType.MESH
WIDTHS = (128, 128, 128, 128, 128, 128, 128, 128)
STARTS = tuple(sum(WIDTHS[:i]) for i in range(len(WIDTHS)))
SPLIT = (384, 384, 384, 384, 384, 256, 256, 256)
X_DIRECT = ()
ORDER = (3, 2, 1, 0)
TILE = 128
PAIRS = tuple((i, j) for i in range(4) for j in range(i + 1))
BF16, F32 = jnp.bfloat16, jnp.float32


def _rem(a, n):
    return lax.rem(a + 2 * n, n)


def gradient_kernel(
    act, grad, red, gram_out,
    raw_near, raw_own, mine, at, gall, part, fwd, land, kept, own_part,
    gram, gram_half, gsend, gcore, g1, g1land, g2, g2land,
    load_sem, az_send, az_recv, ax_send, ax_recv, ac_send, ac_recv,
    g_send, g_recv, p_send, p_recv, m_send, m_recv,
):
    tok = act.shape[0]
    blk = red.shape[0]
    row = blk // NX
    share = row // NC
    dp, tn = lax.axis_index("dp"), lax.axis_index("tensor")
    zl, y = dp // NY, lax.rem(dp, NY)
    zh, x, c = tn // (NX * NC), lax.rem(tn // NC, NX), lax.rem(tn, NC)
    z = zh * NZ + zl

    def device(dz=0, dy=0, dx=0, dc=0):
        pz = _rem(z + dz, 2 * NZ)
        return (
            lax.rem(pz, NZ) * NY + _rem(y + dy, NY),
            (pz // NZ) * NX * NC + _rem(x + dx, NX) * NC + _rem(c + dc, NC),
        )

    def remote(src, dst, send, recv, to):
        return pltpu.make_async_remote_copy(
            src_ref=src, dst_ref=dst, send_sem=send, recv_sem=recv, device_id=to, device_id_type=MESH
        )

    def arrival(dst, recv):
        return remote(dst, dst, recv, recv, device(dc=1))

    line = jnp.where(zl < 2, 2, -2)
    far = -line
    near = 1 - 2 * lax.rem(zl, 2)
    even_y = 1 - 2 * lax.rem(y, 2)
    back_y = NY - 1 - 2 * y

    def row_block(dz2, dy1, r):
        rz = _rem(zl + 2 * dz2, NZ)
        ry = y + even_y * dy1
        rz = rz + (1 - 2 * lax.rem(rz, 2)) * (r % 2)
        ry = ry + (NY - 1 - 2 * ry) * (r // 2)
        return rz * NY + ry

    sources = ((1, 0), (0, 1), (1, 1))
    near_load = {}
    for r in ORDER:
        for i, (dz2, dy1) in enumerate(sources):
            col = row_block(dz2, dy1, r) * blk + x * row
            cp = pltpu.make_async_copy(
                act.at[:, pl.ds(pl.multiple_of(col, 128), row)], raw_near.at[r * 3 + i], load_sem.at[r * 3 + i]
            )
            cp.start()
            near_load[r, i] = cp
    own_load = []
    for r in range(NY):
        col = row_block(0, 0, r) * blk
        cp = pltpu.make_async_copy(act.at[:, pl.ds(pl.multiple_of(col, 128), blk)], raw_own.at[r], load_sem.at[12 + r])
        cp.start()
        own_load.append(cp)
    g_load = []
    for j, (s, wd) in enumerate(zip(STARTS, WIDTHS)):
        cp = pltpu.make_async_copy(grad.at[:, pl.ds(s, wd)], gall.at[j, pl.ds(0, tok), pl.ds(0, wd)], load_sem.at[16 + j])
        cp.start()
        g_load.append(cp)

    barrier = pltpu.get_barrier_semaphore()
    peers = [device(dz=d) for d in (2, -2, 4)] + [device(dz=d, dy=even_y) for d in (2, -2)]
    peers += [device(dz=near), device(dy=even_y), device(dy=back_y)]
    peers += [device(dx=d) for d in (1, 2, 3)] + [device(dc=1)]
    for p in peers:
        pl.semaphore_signal(barrier, inc=1, device_id=p, device_id_type=MESH)
    pl.semaphore_wait(barrier, len(peers))

    sent = []

    def g_copy(j, src, dst, to):
        cols = pl.ds(0, WIDTHS[j])
        cp = remote(
            gall.at[j, pl.ds(src * tok, tok), cols], gall.at[j, pl.ds(dst * tok, tok), cols],
            g_send.at[j, dst], g_recv.at[j, dst], to,
        )
        cp.start()
        sent.append(cp)

    def g_own(j):
        g_load[j].wait()
        g_copy(j, 0, 1, device(dz=line))
        g_copy(j, 0, 2, device(dy=even_y))

    def g_wait(j, slot):
        arrival(gall.at[j, pl.ds(slot * tok, tok), pl.ds(0, WIDTHS[j])], g_recv.at[j, slot]).wait_recv()

    def g_pass(j):
        g_wait(j, 1)
        g_copy(j, 1, 3, device(dy=even_y))

    def g_rest(j):
        g_wait(j, 2)
        g_wait(j, 3)

    def columns(i):
        return pl.ds((i + 1) * tok, tok)

    def a_send(r):
        for i, (dz2, dy1) in enumerate(sources):
            near_load[r, i].wait()
            mine[r * 3 + i] = raw_near[r * 3 + i].T
            cp = remote(
                mine.at[r * 3 + i, pl.ds(pl.multiple_of(c * share, share), share)], at.at[r, x, c, :, columns(i)],
                az_send.at[r * 3 + i], az_recv.at[r * 3 + i], device(dz=far * dz2, dy=even_y * dy1),
            )
            cp.start()
            sent.append(cp)

    def a_share(r, i):
        piece = at.at[r, x, c, :, columns(i)]
        arrival(piece, az_recv.at[r * 3 + i]).wait_recv()
        for k, d in enumerate((1, -1, 2) if r in X_DIRECT else (1, -1)):
            cp = remote(piece, piece, ax_send.at[r * 3 + i, k], ax_recv.at[r * 3 + i, k], device(dx=d))
            cp.start()
            sent.append(cp)

    def a_relay(r, i):
        for k, d in enumerate((1, -1)):
            origin = _rem(x - d, NX)
            arrival(at.at[r, origin, c, :, columns(i)], ax_recv.at[r * 3 + i, k]).wait_recv()
            if r in X_DIRECT:
                continue
            piece = at.at[r, origin, c, pl.ds(k * (share // 2), share // 2), columns(i)]
            cp = remote(piece, piece, ax_send.at[r * 3 + i, 2 + k], ax_recv.at[r * 3 + i, 2 + k], device(dx=d))
            cp.start()
            sent.append(cp)

    def a_core(r):
        origin = _rem(x + 2, NX)
        for i in range(3):
            if r in X_DIRECT:
                arrival(at.at[r, origin, c, :, columns(i)], ax_recv.at[r * 3 + i, 2]).wait_recv()
                continue
            for k in range(2):
                piece = at.at[r, origin, c, pl.ds(k * (share // 2), share // 2), columns(i)]
                arrival(piece, ax_recv.at[r * 3 + i, 2 + k]).wait_recv()
        piece = at.at[r, :, c, :, pl.ds(tok, 3 * tok)]
        cp = remote(piece, piece, ac_send.at[r], ac_recv.at[r], device(dc=1))
        cp.start()
        sent.append(cp)

    def a_wait(r):
        arrival(at.at[r, :, 1 - c, :, pl.ds(tok, 3 * tok)], ac_recv.at[r]).wait_recv()

    z_peer, y_peer = device(dz=near), device(dy=back_y)

    def p_copy(j, k, src, dst, to):
        cp = remote(src, dst, p_send.at[j, k], p_recv.at[j, k], to)
        cp.start()
        sent.append(cp)

    def parts(j):
        return pl.ds(0, SPLIT[j]), pl.ds(SPLIT[j], blk - SPLIT[j])

    def product(j, r):
        cols = pl.ds(0, WIDTHS[j])
        (top, low), cut = parts(j), SPLIT[j]
        value = jnp.dot(at[r].reshape(blk, NZ * tok), gall[j, :, cols], preferred_element_type=F32)
        if r == 0:
            own_part[j, :, cols] = value
        elif r == 3:
            part[j, 2, :, cols] = value.astype(BF16)
            p_copy(j, 0, part.at[j, 2, top, cols], fwd.at[j, 0, top, cols], y_peer)
            p_copy(j, 1, part.at[j, 2, low, cols], fwd.at[j, 1, pl.ds(0, blk - cut), cols], z_peer)
        elif r == 2:
            part[j, 1, top, cols] = value[:cut].astype(BF16)
            kept[j, 1, 0:blk - cut, cols] = value[cut:]
            p_copy(j, 2, part.at[j, 1, top, cols], land.at[j, 1, top, cols], y_peer)
        else:
            part[j, 0, low, cols] = value[cut:].astype(BF16)
            kept[j, 0, top, cols] = value[:cut]
            p_copy(j, 3, part.at[j, 0, low, cols], land.at[j, 0, low, cols], z_peer)

    def p_pass(j, k):
        cols = pl.ds(0, WIDTHS[j])
        rows, to = (parts(j)[k], (z_peer, y_peer)[k])
        held = pl.ds(0, (SPLIT[j], blk - SPLIT[j])[k])
        arrival(fwd.at[j, k, held, cols], p_recv.at[j, k]).wait_recv()
        part[j, k, rows, cols] = (kept[j, k, held, cols] + fwd[j, k, held, cols].astype(F32)).astype(BF16)
        p_copy(j, 4 + k, part.at[j, k, rows, cols], land.at[j, k, rows, cols], to)

    def finish(j):
        wd = WIDTHS[j]
        cols = pl.ds(0, wd)
        top, low = parts(j)
        for k, side, rows in ((2, 1, top), (3, 0, low), (4, 0, top), (5, 1, low)):
            arrival(land.at[j, side, rows, cols], p_recv.at[j, k]).wait_recv()
        total = own_part[j, :, cols] + land[j, 0, :, cols].astype(F32) + land[j, 1, :, cols].astype(F32)
        red[:, STARTS[j]:STARTS[j] + wd] = total.astype(BF16)
        half = red[:, STARTS[j]:STARTS[j] + wd]
        for i in range(blk // TILE):
            term = lax.dot_general(
                half[i * TILE:(i + 1) * TILE], half[:(i + 1) * TILE], (((1,), (1,)), ((), ())), preferred_element_type=F32
            )
            for k in range(i + 1):
                at_row = PAIRS.index((i, k)) * TILE
                tile = term[:, k * TILE:(k + 1) * TILE]
                if j == 0:
                    gram[at_row:at_row + TILE] = tile
                else:
                    gram[at_row:at_row + TILE] += tile

    def turn_own(r):
        own_load[r].wait()
        at[r, :, :, :, 0:tok] = raw_own[r].T.reshape(NX, NC, share, tok)

    n = len(WIDTHS)
    g_own(0)
    g_own(1)
    a_send(3)
    a_send(2)
    a_send(1)
    turn_own(3)
    turn_own(2)
    turn_own(1)
    turn_own(0)
    a_share(3, 0)
    a_share(3, 1)
    g_pass(0)
    g_own(2)
    a_share(3, 2)
    a_relay(3, 0)
    a_share(2, 1)
    a_share(2, 0)
    a_relay(3, 1)
    g_pass(1)
    g_own(3)
    a_share(2, 2)
    a_relay(3, 2)
    a_share(1, 1)
    a_share(1, 0)
    a_relay(2, 1)
    g_pass(2)
    g_own(4)
    a_relay(2, 0)
    a_share(1, 2)
    a_relay(2, 2)
    a_core(3)
    a_relay(1, 1)
    g_pass(3)
    g_own(5)
    a_send(0)
    a_relay(1, 0)
    g_rest(0)
    a_wait(3)
    product(0, 3)
    g_rest(1)
    product(1, 3)
    a_relay(1, 2)
    a_core(2)
    g_pass(4)
    g_own(6)
    a_wait(2)
    product(0, 2)
    a_core(1)
    product(1, 2)
    g_rest(2)
    product(2, 3)
    a_share(0, 0)
    product(2, 2)
    p_pass(0, 1)
    a_wait(1)
    product(0, 1)
    g_pass(5)
    g_own(7)
    product(1, 1)
    product(2, 1)
    p_pass(0, 0)
    p_pass(1, 0)
    p_pass(1, 1)
    g_rest(3)
    product(3, 3)
    a_relay(0, 0)
    p_pass(2, 1)
    product(3, 1)
    product(3, 2)
    g_pass(6)
    a_share(0, 1)
    p_pass(2, 0)
    a_share(0, 2)
    g_rest(4)
    product(4, 3)
    g_pass(7)
    a_relay(0, 1)
    product(4, 1)
    product(4, 2)
    a_relay(0, 2)
    p_pass(3, 0)
    p_pass(3, 1)
    g_rest(5)
    product(5, 3)
    product(5, 1)
    product(5, 2)
    a_core(0)
    p_pass(4, 1)
    p_pass(4, 0)
    g_rest(6)
    product(6, 3)
    product(6, 1)
    product(6, 2)
    a_wait(0)
    product(0, 0)
    product(1, 0)
    g_rest(7)
    product(7, 3)
    product(7, 1)
    p_pass(5, 1)
    product(7, 2)
    product(2, 0)
    product(3, 0)
    p_pass(5, 0)
    product(4, 0)
    finish(0)
    product(5, 0)
    finish(1)
    product(6, 0)
    finish(2)
    product(7, 0)
    finish(3)
    finish(4)
    p_pass(6, 0)
    p_pass(6, 1)
    p_pass(7, 0)
    p_pass(7, 1)
    finish(5)
    finish(6)
    finish(7)

    half_rows = gram.shape[0] // 2
    piece = half_rows // NX
    gsend[...] = gram[...].astype(BF16)
    other = remote(
        gsend.at[pl.ds(pl.multiple_of((1 - c) * half_rows, 128), half_rows)], gcore,
        m_send.at[0], m_recv.at[0], device(dc=1),
    )
    other.start()
    sent.append(other)
    other.wait_recv()
    mid = gram[pl.ds(pl.multiple_of(c * half_rows, 128), half_rows), :] + gcore[...].astype(F32)
    gram[0:half_rows, :] = mid
    g1[...] = mid.astype(BF16)
    for k, d in enumerate((2, 1, 3)):
        rows = pl.multiple_of(_rem(x + d, NX) * piece, 32)
        cp = remote(g1.at[pl.ds(rows, piece)], g1land.at[k], m_send.at[1 + k], m_recv.at[1 + k], device(dx=d))
        cp.start()
        sent.append(cp)
    own_rows = pl.multiple_of(x * piece, 32)
    for k in range(3):
        arrival(g1land.at[k], m_recv.at[1 + k]).wait_recv()
    low = gram[pl.ds(own_rows, piece), :]
    low = low + g1land[0].astype(F32) + g1land[1].astype(F32) + g1land[2].astype(F32)
    g2[...] = low.astype(BF16)
    cp = remote(g2, g2land, m_send.at[4], m_recv.at[4], device(dz=4))
    cp.start()
    sent.append(cp)
    cp.wait_recv()
    final_rows = pl.multiple_of(c * half_rows + x * piece, 32)
    final = gram_half.at[pl.ds(final_rows, piece)]
    gram_half[pl.ds(final_rows, piece), :] = (g2[...].astype(F32) + g2land[...].astype(F32)).astype(BF16)
    for k, d in enumerate((2, 1, 3)):
        cp = remote(final, final, m_send.at[5 + k], m_recv.at[5 + k], device(dx=d))
        cp.start()
        sent.append(cp)
    cp = remote(final, final, m_send.at[8], m_recv.at[8], device(dc=1))
    cp.start()
    sent.append(cp)
    for k, d in ((1, 1), (2, 3), (0, 2)):
        rows = pl.multiple_of(c * half_rows + _rem(x - d, NX) * piece, 32)
        slot = gram_half.at[pl.ds(rows, piece)]
        arrival(slot, m_recv.at[5 + k]).wait_recv()
        cp = remote(slot, slot, m_send.at[9 + k], m_recv.at[9 + k], device(dc=1))
        cp.start()
        sent.append(cp)
    for k, d in ((-1, 0), (1, 1), (2, 3), (0, 2)):
        rows = pl.multiple_of((1 - c) * half_rows + _rem(x - d, NX) * piece, 32)
        arrival(gram_half.at[pl.ds(rows, piece)], m_recv.at[9 + k]).wait_recv()
    gram_out[...] = gram_half[...]

    for cp in sent:
        cp.wait_send()


def gradient_call(act, grad, blk):
    tok, ff = grad.shape
    n, wide = len(WIDTHS), max(WIDTHS)
    row = blk // NX
    packed = len(PAIRS) * TILE
    dma = pltpu.SemaphoreType.DMA
    flops = 2 * tok * NZ * blk * NY * ff + 2 * blk * blk * ff
    return pl.pallas_call(
        gradient_kernel,
        out_shape=(pltpu.VMEM((blk, ff), BF16), pltpu.VMEM((packed, TILE), BF16)),
        in_specs=[pl.BlockSpec(memory_space=pl.ANY)] * 2,
        out_specs=[pl.BlockSpec(memory_space=pltpu.VMEM)] * 2,
        scratch_shapes=[
            pltpu.VMEM((12, tok, row), BF16),
            pltpu.VMEM((NY, tok, blk), BF16),
            pltpu.VMEM((12, row, tok), BF16),
            pltpu.VMEM((NY, NX, NC, row // NC, NZ * tok), BF16),
            pltpu.VMEM((n, NZ * tok, wide), BF16),
            pltpu.VMEM((n, 3, blk, wide), BF16),
            pltpu.VMEM((n, 2, max(SPLIT), wide), BF16),
            pltpu.VMEM((n, 2, blk, wide), BF16),
            pltpu.VMEM((n, 2, max(SPLIT), wide), F32),
            pltpu.VMEM((n, blk, wide), F32),
            pltpu.VMEM((packed, TILE), F32),
            pltpu.VMEM((packed, TILE), BF16),
            pltpu.VMEM((packed, TILE), BF16),
            pltpu.VMEM((packed // 2, TILE), BF16),
            pltpu.VMEM((packed // 2, TILE), BF16),
            pltpu.VMEM((3, packed // 8, TILE), BF16),
            pltpu.VMEM((packed // 8, TILE), BF16),
            pltpu.VMEM((packed // 8, TILE), BF16),
            dma((16 + n,)), dma((12,)), dma((12,)), dma((12, 4)), dma((12, 4)), dma((NY,)), dma((NY,)),
            dma((n, 4)), dma((n, 4)), dma((n, 6)), dma((n, 6)), dma((12,)), dma((12,)),
        ],
        compiler_params=pltpu.CompilerParams(
            collective_id=0, has_side_effects=True, vmem_limit_bytes=56 * 2**20
        ),
        cost_estimate=pl.CostEstimate(flops=flops, bytes_accessed=8 * 2**20, transcendentals=0),
        name="gradient",
    )(act, grad)


def _mm(a, b):
    return jnp.dot(a.astype(BF16), b.astype(BF16), preferred_element_type=F32)


def root_kernel(refresh, gram, left, old, red, stats, roots, update, state, root, square, pair):
    blk = left.shape[0]
    me = lax.axis_index("dp")
    for k, (i, j) in enumerate(PAIRS):
        term = (1.0 / FF) * gram[k * TILE:(k + 1) * TILE].astype(F32)
        rows, cols = slice(i * TILE, (i + 1) * TILE), slice(j * TILE, (j + 1) * TILE)
        stats[rows, cols] = STAT_DECAY * left[rows, cols] + term
        if i != j:
            stats[cols, rows] = STAT_DECAY * left[cols, rows] + term.T
    picked = refresh[0] == me
    for i in range(1, refresh.shape[0]):
        picked = picked | (refresh[i] == me)

    @pl.when(picked)
    def _():
        value = stats[...]
        norm = blk * jnp.sqrt(jnp.mean(value * value, keepdims=True) + 1e-6)
        scale = jnp.exp(-0.25 * jnp.log(norm))
        state[...] = value * (0.25 / norm)
        eye = (
            lax.broadcasted_iota(jnp.int32, (blk, blk), 0) == lax.broadcasted_iota(jnp.int32, (blk, blk), 1)
        ).astype(F32)
        root[...] = scale * (1.25 * eye - state[...])
        pair[0:blk] = state[...].astype(BF16)
        for i in range(ITERS - 1):
            half = pair[0:blk]
            if i == 0:
                square[...] = jnp.dot(half, half, preferred_element_type=F32)
            else:
                pair[blk:] = root[...].astype(BF16)
                both = jnp.dot(pair[...], half, preferred_element_type=F32)
                square[...] = both[0:blk]
                root[...] = 1.25 * root[...] - both[blk:]
            cube = jnp.dot(half, square[...].astype(BF16), preferred_element_type=F32)
            cube = 9.375 * state[...] - 5.0 * square[...] + cube
            last = _mm(square[...], cube)
            value = 2.44140625 * state[...] - 7.8125 * square[...] + last
            state[...] = value
            pair[0:blk] = value.astype(BF16)
        root[...] = 1.25 * root[...] - _mm(root[...], pair[0:blk])
        roots[...] = root[...]

    @pl.when(jnp.logical_not(picked))
    def _():
        roots[...] = old[...]

    update[...] = jnp.dot(roots[...].astype(BF16), red[...], preferred_element_type=F32).astype(BF16)


def root_call(refresh, gram, left, old, red):
    blk, ff = red.shape
    vmem = pl.BlockSpec(memory_space=pltpu.VMEM)
    return pl.pallas_call(
        root_kernel,
        out_shape=(
            jax.ShapeDtypeStruct((blk, blk), F32),
            jax.ShapeDtypeStruct((blk, blk), F32),
            jax.ShapeDtypeStruct((blk, ff), BF16),
        ),
        in_specs=[pl.BlockSpec(memory_space=pltpu.SMEM)] + [vmem] * 4,
        out_specs=[vmem] * 3,
        scratch_shapes=[pltpu.VMEM((blk, blk), F32)] * 3 + [pltpu.VMEM((2 * blk, blk), BF16)],
        compiler_params=pltpu.CompilerParams(vmem_limit_bytes=40 * 2**20),
        name="root",
    )(refresh, gram, left, old, red)


def per_device(activations, out_grads, left_stats, old_roots, refresh):
    reduced, gram = gradient_call(activations, out_grads, left_stats.shape[1])
    return root_call(refresh, gram, left_stats, old_roots, reduced)


def solution(mesh):
    placed = (P("dp", None), P("dp", "tensor"), P("dp", None), P("dp", None), P())
    return jax.shard_map(
        per_device,
        mesh=mesh,
        in_specs=placed,
        out_specs=(P("dp", None), P("dp", None), P("dp", "tensor")),
        check_vma=False,
    )
```
